128 devices in a mesh: loop: 32 (over x, z, y_lo), feat: 4 (over y_hi, core).
Axes of the slice: x: 4, y: 4 (y_hi: 2, y_lo: 2; y = y_hi * 2 + y_lo), z: 4, core: 2. Of those that a mesh axis runs over, the one named last changes fastest.
Arguments:
- features: bfloat16 [262144, 128], P('loop', 'feat'), may hold values from -6 to 6
- band_blocks: bfloat16 [2048, 3, 128, 128], P('loop'), may hold values from 0 to 1.5, as said below
- off_blocks: bfloat16 [2048, 128, 128], P('loop'), may hold values from 0 to 1.5, as said below
- off_row: int32 [2048], P('loop'), may hold values from 0 to 63
- off_col: int32 [2048], P('loop'), may hold values from 0 to 63
- off_part: int32 [2048, 1], P('loop'), may hold values from 0 to 31; in each aligned block of 64 rows (0 to 63, 64 to 127, ...) at most 4 rows name the same one
- w_self: bfloat16 [128, 256], P('feat'), may hold values from -0.5 to 0.5
- w_neigh: bfloat16 [128, 256], P('feat'), may hold values from -4 to 4
- bias: float32 [256], P('feat'), may hold values from -3 to 3
- cotangent: bfloat16 [262144, 256], P('loop', 'feat'), may hold values from -6 to 6
Outputs:
- hidden: bfloat16 [262144, 256], P('loop', 'feat')
- grad_features: bfloat16 [262144, 128], P('loop', 'feat')
- weight_grads: float32 [2, 128, 256], P(None, 'feat')
- bias_grad: float32 [256], P('feat')
The draws below stay inside these ranges and needn't reach their ends.
Inputs may be any that keep to these rules, and one draw needn't show every extreme that they name: `band_blocks`: nonnegative edge weights; zero or between 0.5 and 1.5. `off_blocks`: nonnegative edge weights; zero or between 0.5 and 1.5. `off_part`: off-band block g belongs to partition g // 64; among the blocks of one partition at most 4 have their columns in any one partition.
All inputs are finite; a program needn't handle non-finite values.
Results may differ from the reference program's by a relative error of at most 0.007.
Values may be sent and summed in bfloat16 or wider, within the bound.
No kernel may reach another device: no remote copies, remote signals or barrier semaphores. Data moves between devices by JAX's collectives and lax.ppermute only.
A program may use at most 128 MiB of HBM per device.

```python
import math
import jax
import jax.numpy as jnp
import numpy as np

F = 128
H = 256
BLK = 128
ROWS_DEV = 8192
KOFF = 64
CAP = 4
NODES = 262144
NBLK = 2048
OFF_BLOCKS = 2048
N_LOOP = 32


def sparse_weights(key, shape):
    keep = jax.random.bernoulli(jax.random.fold_in(key, 1), 0.3, shape)
    value = jax.random.uniform(jax.random.fold_in(key, 2), shape, jnp.float32, 0.5, 1.5)
    return jnp.where(keep, value, 0.0)


def draw_band_blocks(key, part):
    key = jax.random.fold_in(key, 11)
    return sparse_weights(key, (NBLK, 3, BLK, BLK)).astype(jnp.bfloat16)


def draw_off_blocks(key, part):
    key = jax.random.fold_in(key, 23)
    return sparse_weights(key, (OFF_BLOCKS, BLK, BLK)).astype(jnp.bfloat16)


def with_ends(result, rng, low, largest):
    longest = result.shape.index(max(result.shape))
    spots = []
    for shift in (0, 1):
        where = [jax.random.randint(jax.random.fold_in(rng, axis), (), 0, length) for axis, length in enumerate(result.shape)]
        where[longest] = (where[longest] + shift) % result.shape[longest]
        spots.append(tuple(where))
    return result.at[spots[0]].set(low).at[spots[1]].set(largest)


def block_levels(own_key, shape, split, smallest, top_value):
    gain = 1.0
    for dim, blocks in split:
        steps = jax.random.uniform(jax.random.fold_in(jax.random.fold_in(own_key, 6), dim), (blocks,), jnp.float32, smallest / len(split), top_value / len(split))
        gain = gain * jnp.repeat(jnp.exp(steps), shape[dim] // blocks).reshape((-1,) + (1,) * (len(shape) - 1 - dim))
    return gain


def deal_out(own_key, own, number, rows, amount, top, most, skew):
    sequence = jax.random.permutation(own_key, amount)
    crowded, usual = load_shares(amount, rows * top, most, skew, True), load_shares(amount, rows * top, most, skew, False)
    places = jnp.arange(amount)

    def named(lengths, rotation):
        used = int((lengths > 0).sum())
        fixed = max(1, used // 4)
        passed = fixed + (places - fixed + rotation * (used - fixed)) % max(1, amount - fixed)
        return jnp.zeros((amount,), jnp.int32).at[sequence[jnp.where(places < fixed, places, passed)]].set(jnp.asarray(lengths, jnp.int32))

    lengths = jnp.where(number % 4 == 0, named(crowded, number // 4), named(usual, number - number // 4 - 1))
    mixed = jax.random.permutation(jax.random.fold_in(own, 3), amount)
    source_of, sink = mixed[0:amount // 2 * 2:2], mixed[1:amount // 2 * 2:2]
    slack = jnp.minimum(lengths[source_of] - 1, most - lengths[sink]) // 2
    slack = jnp.where((source_of == sequence[0]) | (sink == sequence[0]) | (lengths[sink] == 0), 0, jnp.maximum(slack, 0))
    passed = jax.random.randint(jax.random.fold_in(own, 4), (amount // 2,), 0, 1 << 20) % (slack + 1)
    lengths = lengths.at[source_of].add(-passed).at[sink].add(passed)
    items = jnp.searchsorted(jnp.cumsum(lengths), jnp.arange(rows * top), side="right").astype(jnp.int32)
    table = items.reshape(top, rows).T
    table = table[jax.random.permutation(jax.random.fold_in(own, 1), rows)]
    rotation = jax.random.randint(jax.random.fold_in(own, 2), (rows, 1), 0, top)
    return jnp.take_along_axis(table, (jnp.arange(top)[None, :] + rotation) % top, axis=1)


def load_shares(number_of, total, reach, lean, full):
    weights = [(1 << 20) // math.isqrt(rank ** lean) + 1 for rank in range(1, number_of + 1)]
    largest = reach if full else min(reach, max(-(-total // number_of), total * weights[0] // sum(weights)))
    least = 1 if total - largest >= number_of - 1 else 0
    given, surplus = [largest] + [least] * (number_of - 1), total - largest - least * (number_of - 1)
    while surplus > 0:
        movable = [i for i in range(1, number_of) if given[i] < largest] or [i for i in range(1, number_of) if given[i] < reach]
        whole, remaining = sum([weights[i] for i in movable]), surplus
        for i in movable:
            extra = min(reach - given[i], max(1, remaining * weights[i] // whole), surplus)
            given[i] = given[i] + extra
            surplus = surplus - extra
    return np.array(given)


def normal_values(rng, extent, scale, limit, shards=(), held_as=jnp.bfloat16):
    values = scale * jax.random.normal(rng, extent, jnp.float32)
    if shards:
        values = values * block_levels(rng, extent, shards, -0.22, 0.18)
    return jnp.clip(values, -limit, limit).astype(held_as)


def setup_inputs(seed: int = 0) -> dict:
    key_list = jax.random.split(jax.random.key(seed), 11)
    features = normal_values(key_list[0], (NODES, F), 1.0, 6.0, ((0, 32), (1, 4)))
    band_blocks = draw_band_blocks(jax.random.fold_in(key_list[10], 71), 0)
    off_blocks = draw_off_blocks(jax.random.fold_in(key_list[10], 71), 0)
    off_row = with_ends(jax.random.randint(key_list[3], (OFF_BLOCKS,), 0, ROWS_DEV // BLK), jax.random.fold_in(key_list[3], 1), 0, (ROWS_DEV // BLK) - 1).astype(jnp.int32)
    off_col = with_ends(jax.random.randint(key_list[4], (OFF_BLOCKS,), 0, ROWS_DEV // BLK), jax.random.fold_in(key_list[4], 1), 0, (ROWS_DEV // BLK) - 1).astype(jnp.int32)
    off_part_keys = jax.random.split(jax.random.fold_in(key_list[5], 1), OFF_BLOCKS // KOFF)
    off_part_turns = jax.random.permutation(jax.random.fold_in(key_list[5], 3), OFF_BLOCKS // KOFF)
    off_part = jax.vmap(lambda own, number: deal_out(jax.random.fold_in(key_list[5], 2), own, number, KOFF, N_LOOP, 1, CAP, 2))(off_part_keys, off_part_turns).reshape((OFF_BLOCKS, 1))
    w_self = normal_values(key_list[6], (F, H), F ** -0.5, 0.5, ((0, 4),))
    w_neigh = normal_values(key_list[7], (F, H), (F // 64) ** -0.5, 4.0, ((0, 4),))
    bias = normal_values(key_list[8], (H,), 0.5, 3.0, ((0, 4),), jnp.float32)
    cotangent = normal_values(key_list[9], (NODES, H), 1.0, 6.0, ((0, 32), (1, 4)))
    return dict(features=features, band_blocks=band_blocks, off_blocks=off_blocks, off_row=off_row, off_col=off_col, off_part=off_part, w_self=w_self, w_neigh=w_neigh, bias=bias, cotangent=cotangent)


def reference(features, band_blocks, off_blocks, off_row, off_col, off_part, w_self, w_neigh, bias, cotangent):
    row_blocks = ROWS_DEV // BLK
    owner = jnp.arange(OFF_BLOCKS, dtype=jnp.int32) // KOFF
    row_global = (owner * row_blocks + off_row).astype(jnp.int32)
    col_global = (off_part[:, 0] * row_blocks + off_col).astype(jnp.int32)
    band_weights = band_blocks.astype(jnp.float32)
    off_weights = off_blocks.astype(jnp.float32)
    degree = 1.0 + jnp.sum(band_weights, axis=(1, 3)) + jax.ops.segment_sum(jnp.sum(off_weights, axis=2), row_global, NBLK)
    inverse = 1.0 / degree
    feature_blocks = features.astype(jnp.float32).reshape(NBLK, BLK, F)
    stacked = jnp.stack([jnp.roll(feature_blocks, 1, 0), feature_blocks, jnp.roll(feature_blocks, -1, 0)], 1)
    aggregate = jnp.einsum("bokj,bojf->bkf", band_weights, stacked)
    off_terms = jnp.einsum("gkj,gjf->gkf", off_weights, feature_blocks[col_global])
    aggregate = aggregate + jax.ops.segment_sum(off_terms, row_global, NBLK)
    mean_feat = (aggregate * inverse[:, :, None]).astype(jnp.bfloat16).reshape(NODES, F)
    pre = jnp.dot(features, w_self, preferred_element_type=jnp.float32) + jnp.dot(mean_feat, w_neigh, preferred_element_type=jnp.float32) + bias
    sigmoid_pre = jax.nn.sigmoid(pre)
    hidden = (pre * sigmoid_pre).astype(jnp.bfloat16)
    grad_pre = (cotangent.astype(jnp.float32) * sigmoid_pre * (1.0 + pre * (1.0 - sigmoid_pre))).astype(jnp.bfloat16)
    grad_scale = 1.0 / (NODES ** 0.5)
    weight_grads = jnp.stack([jnp.dot(features.T, grad_pre, preferred_element_type=jnp.float32), jnp.dot(mean_feat.T, grad_pre, preferred_element_type=jnp.float32)]) * grad_scale
    bias_grad = jnp.sum(grad_pre.astype(jnp.float32), axis=0) * grad_scale
    back_mean = (jnp.dot(grad_pre, w_neigh.T, preferred_element_type=jnp.float32).reshape(NBLK, BLK, F) * inverse[:, :, None]).astype(jnp.bfloat16)
    back_blocks = back_mean.astype(jnp.float32)
    terms = jnp.einsum("bokj,bkf->bojf", band_weights, back_blocks)
    band_back = jnp.roll(terms[:, 0], -1, 0) + terms[:, 1] + jnp.roll(terms[:, 2], 1, 0)
    off_back = jnp.einsum("gkj,gkf->gjf", off_weights, back_blocks[row_global])
    band_back = band_back + jax.ops.segment_sum(off_back, col_global, NBLK)
    self_part = jnp.dot(grad_pre, w_self.T, preferred_element_type=jnp.float32)
    grad_features = (self_part + band_back.reshape(NODES, F)).astype(jnp.bfloat16)
    return hidden, grad_features, weight_grads, bias_grad
```

```python
import math

import jax
import jax.numpy as jnp
from jax import lax
from jax.experimental import pallas as pl
from jax.experimental.pallas import tpu as pltpu
from jax.sharding import PartitionSpec as P

BF = jnp.bfloat16
F32 = jnp.float32
BLK = 128
ONES = 16
CAP = 4
NT = (((1,), (1,)), ((), ()))
TN = (((0,), (0,)), ((), ()))


def params(mib=40):
    return pltpu.CompilerParams(vmem_limit_bytes=mib * 1024 * 1024)


def full(shape):
    return pl.BlockSpec(shape, lambda *_: (0,) * len(shape))


def lanes(block, width=BLK):
    return pl.ds(pl.multiple_of(block * BLK, BLK), width)


def dot(a, b, dims=(((1,), (0,)), ((), ()))):
    return lax.dot_general(a, b, dims, preferred_element_type=F32)


def slots_kernel(part_ref, col_ref, key_ref, request_ref):
    part, col = part_ref[...], col_ref[...]
    count = part.shape[1]
    first = lax.broadcasted_iota(jnp.int32, (count, count), 0)
    second = lax.broadcasted_iota(jnp.int32, (count, count), 1)
    part_down = jnp.sum(jnp.where(first == second, part, 0), axis=1, keepdims=True)
    earlier = (part_down == part) & (first < second)
    slot = jnp.sum(earlier.astype(jnp.int32), axis=0, keepdims=True)
    key_ref[...] = part * CAP + slot
    shape = request_ref.shape
    wide = (shape[0], shape[1], count)
    owner = lax.broadcasted_iota(jnp.int32, wide, 0)
    lane = lax.broadcasted_iota(jnp.int32, shape, 2)
    hit = owner == part[None]
    table = jnp.zeros(shape, jnp.int32)
    for s in range(CAP):
        value = jnp.sum(
            jnp.where(hit & (slot[None] == s), col[None], 0), axis=2, keepdims=True
        )
        table = jnp.where(lane == s, value, table)
    request_ref[...] = table


def slots(part, col, loop_size):
    count = part.shape[1]
    return pl.pallas_call(
        slots_kernel,
        out_shape=(
            jax.ShapeDtypeStruct((1, count), jnp.int32),
            jax.ShapeDtypeStruct((loop_size, 8, BLK), jnp.int32),
        ),
        name="slots",
    )(part, col)


def answer_kernel(asked_ref, x_ref, out_ref, table, sem):
    copy = pltpu.make_async_copy(asked_ref.at[:, 0, :], table, sem)
    copy.start()
    copy.wait()

    def body(p, carry):
        for s in range(CAP):
            out_ref[p, s] = x_ref[:, lanes(table[p, s])]
        return carry

    lax.fori_loop(0, out_ref.shape[0], body, 0, unroll=4)


def answers(asked, x):
    loop_size, cols = asked.shape[0], x.shape[0]
    return pl.pallas_call(
        answer_kernel,
        in_specs=[pl.BlockSpec(memory_space=pl.ANY), pl.BlockSpec(memory_space=pltpu.VMEM)],
        out_shape=jax.ShapeDtypeStruct((loop_size, CAP, cols, BLK), BF),
        scratch_shapes=[pltpu.SMEM((loop_size, BLK), jnp.int32), pltpu.SemaphoreType.DMA],
        compiler_params=params(),
        name="answers",
    )(asked, x)


def band_kernel(x_ref, low_ref, high_ref, a_ref, out_ref, wide):
    step = pl.program_id(0)
    cols, rows = x_ref.shape

    @pl.when(step == 0)
    def _():
        wide[0:cols, 0:BLK] = low_ref[...]
        wide[0:cols, BLK : BLK + rows] = x_ref[...]
        wide[0:cols, BLK + rows :] = high_ref[...]
        wide[cols:, :] = jnp.ones((ONES, wide.shape[1]), BF)

    group = a_ref.shape[0]
    for r in range(group):
        left = wide[:, lanes(step * group + r, 3 * BLK)]
        right = jnp.concatenate([a_ref[r, 0], a_ref[r, 1], a_ref[r, 2]], axis=1)
        out_ref[:, r * BLK : (r + 1) * BLK] = dot(left, right, NT)


def band_forward(x, low, high, band):
    cols, rows = x.shape
    blocks, group = band.shape[0], 8
    return pl.pallas_call(
        band_kernel,
        grid=(blocks // group,),
        in_specs=[
            full((cols, rows)),
            full((cols, BLK)),
            full((cols, BLK)),
            pl.BlockSpec((group, 3, BLK, BLK), lambda i: (i, 0, 0, 0)),
        ],
        out_specs=pl.BlockSpec((cols + ONES, group * BLK), lambda i: (0, i)),
        out_shape=jax.ShapeDtypeStruct((cols + ONES, rows), F32),
        scratch_shapes=[pltpu.VMEM((cols + ONES, rows + 2 * BLK), BF)],
        compiler_params=params(),
        cost_estimate=pl.CostEstimate(
            flops=2 * 48 * 3 * BLK * rows, bytes_accessed=9 * 1024 * 1024, transcendentals=0
        ),
        name="band_forward",
    )(x, low, high, band)


def off_kernel(row_ref, key_ref, band_ref, panel_ref, a_ref, mean_ref, inverse_ref, total):
    step = pl.program_id(0)
    cols = panel_ref.shape[1]
    group = a_ref.shape[0]

    @pl.when(step == 0)
    def _():
        total[...] = band_ref[...]

    ones = jnp.ones((ONES, BLK), BF)
    for start in range(0, group, 8):
        terms = []
        for r in range(start, start + 8):
            left = jnp.concatenate([panel_ref[key_ref[0, step * group + r]], ones], axis=0)
            terms.append(dot(left, a_ref[r], NT))
        for r in range(start, start + 8):
            where = lanes(row_ref[step * group + r])
            total[:, where] = total[:, where] + terms[r - start]

    @pl.when(step == pl.num_programs(0) - 1)
    def _():
        width = 8 * BLK
        for start in range(0, total.shape[1], width):
            inverse = 1.0 / (1.0 + total[cols : cols + 1, start : start + width])
            inverse_ref[:, start : start + width] = inverse
            mean_ref[:, start : start + width] = (
                total[0:cols, start : start + width] * inverse
            ).astype(BF)


def off_forward(row, key, band_sum, panels, off):
    count, cols = off.shape[0], panels.shape[1]
    rows, group = band_sum.shape[1], 16
    return pl.pallas_call(
        off_kernel,
        grid_spec=pltpu.PrefetchScalarGridSpec(
            num_scalar_prefetch=2,
            grid=(count // group,),
            in_specs=[
                full(band_sum.shape),
                full(panels.shape),
                pl.BlockSpec((group, BLK, BLK), lambda i, *_: (i, 0, 0)),
            ],
            out_specs=[full((cols, rows)), full((1, rows))],
            scratch_shapes=[pltpu.VMEM(band_sum.shape, F32)],
        ),
        out_shape=(
            jax.ShapeDtypeStruct((cols, rows), BF),
            jax.ShapeDtypeStruct((1, rows), F32),
        ),
        compiler_params=params(),
        name="off_forward",
    )(row, key, band_sum, panels, off)


def weights_kernel(feat_ref, w0, w1, w2, w3, down_ref, bias_ref, back_ref):
    feat = feat_ref[0]
    pieces = [w0, w1, w2, w3]
    cols = w0.shape[0] // 2 - 4
    hidden = w0.shape[1]
    part = hidden // 4
    here = lax.broadcasted_iota(jnp.int32, (hidden, hidden), 0)
    there = lax.broadcasted_iota(jnp.int32, (hidden, hidden), 1)
    place = (jnp.bitwise_xor(there // part, feat)) * part + there % part
    chosen = jnp.where(here == place, 1.0, 0.0).astype(BF)
    tall = jnp.concatenate(
        [w[0:cols, :].astype(BF) for w in pieces]
        + [w[cols : 2 * cols, :].astype(BF) for w in pieces],
        axis=0,
    )
    down_ref[...] = (0.5 * dot(chosen, tall, (((0,), (1,)), ((), ())))).astype(BF)
    own = jnp.concatenate([w0[cols : 2 * cols, :].astype(BF), w0[0:cols, :].astype(BF)], axis=0)
    back_ref[...] = dot(own, chosen).astype(BF)
    eye = lax.broadcasted_iota(jnp.int32, (part, part), 0) == lax.broadcasted_iota(
        jnp.int32, (part, part), 1
    )
    for k, w in enumerate(pieces):
        line = w[2 * cols : 2 * cols + 1, 0:part]
        bias_ref[k * part : (k + 1) * part, :] = 0.5 * jnp.sum(
            jnp.where(eye, line, 0.0), axis=1, keepdims=True
        )


def weights(feat, packs):
    hidden = packs[0].shape[1]
    cols = packs[0].shape[0] // 2 - 4
    return pl.pallas_call(
        weights_kernel,
        in_specs=[pl.BlockSpec(memory_space=pltpu.SMEM)]
        + [pl.BlockSpec(memory_space=pltpu.VMEM)] * 4,
        out_shape=(
            jax.ShapeDtypeStruct((hidden, 8 * cols), BF),
            jax.ShapeDtypeStruct((hidden, 1), F32),
            jax.ShapeDtypeStruct((2 * cols, hidden), BF),
        ),
        name="weights",
    )(feat, *packs)


def dense_kernel(
    feat_ref, x0, x1, x2, x3, m0, m1, m2, m3, c0, c1, c2, c3, inverse_ref, down_ref, bias_ref,
    back_w_ref, hidden_ref, back_ref, self_ref, grads_ref, total,
):
    step = pl.program_id(0)
    cols, part = x0.shape[0], c0.shape[0]
    width = 2 * BLK

    @pl.when(step == 0)
    def _():
        total[...] = jnp.zeros_like(total)

    ones = jnp.ones((ONES, width), BF)

    def body(i, carry):
        at = pl.ds(pl.multiple_of(i * width, width), width)
        own = [x0[:, at], m0[:, at]]
        both = jnp.concatenate(
            [own[0], x1[:, at], x2[:, at], x3[:, at], own[1], m1[:, at], m2[:, at], m3[:, at]],
            axis=0,
        )
        half = dot(down_ref[...], both) + bias_ref[...]
        grads = []
        for k, c in enumerate((c0, c1, c2, c3)):
            u = half[k * part : (k + 1) * part]
            t = jnp.tanh(u)
            q = u * t
            if k == 0:
                hidden_ref[:, at] = (u + q).astype(BF)
            grads.append((c[:, at].astype(F32) * (0.5 + 0.5 * t) * (1.0 + u - q)).astype(BF))
        grad = jnp.concatenate(grads, axis=0)
        backs = dot(back_w_ref[...], grad)
        back_ref[:, at] = (backs[0:cols] * inverse_ref[:, at]).astype(BF)
        self_ref[:, at] = backs[cols:]
        total[...] += dot(jnp.concatenate(own + [ones], axis=0), grad, NT)
        return carry

    lax.fori_loop(0, x0.shape[1] // width, body, 0, unroll=2)

    @pl.when(step == pl.num_programs(0) - 1)
    def _():
        feat = feat_ref[0]
        sums = total[0 : 2 * cols, :]
        low, high = sums[:, 0:BLK], sums[:, BLK:]
        far = (feat & 2) != 0
        halves = [jnp.where(far, high, low), jnp.where(far, low, high)]
        halves = [jnp.where((feat & 1) != 0, pltpu.roll(h, part, 1), h) for h in halves]
        groups = 2 * cols // 8
        for r in range(groups):
            for h in range(2):
                grads_ref[2 * r + h] = halves[h][8 * r : 8 * r + 8]
        bias_tile = total[2 * cols : 2 * cols + 8, 0:BLK]
        for r in range(2 * groups, grads_ref.shape[0]):
            grads_ref[r] = bias_tile


def dense(feat, xs, ms, cs, inverse, down, bias, back_w, loop_size):
    cols, rows = xs[0].shape
    part = cs[0].shape[0]
    chunk = 1024
    along = lambda height: pl.BlockSpec((height, chunk), lambda i: (0, i))
    return pl.pallas_call(
        dense_kernel,
        grid=(rows // chunk,),
        in_specs=[pl.BlockSpec(memory_space=pltpu.SMEM)]
        + [along(cols)] * 8
        + [along(part)] * 4
        + [along(1), full(down.shape), full(bias.shape), full(back_w.shape)],
        out_specs=[along(part), along(cols), along(cols), full((loop_size, 8, BLK))],
        out_shape=(
            jax.ShapeDtypeStruct((part, rows), BF),
            jax.ShapeDtypeStruct((cols, rows), BF),
            jax.ShapeDtypeStruct((cols, rows), F32),
            jax.ShapeDtypeStruct((loop_size, 8, BLK), F32),
        ),
        scratch_shapes=[pltpu.VMEM((2 * cols + ONES, 4 * part), F32)],
        compiler_params=params(),
        name="dense",
    )(feat, *xs, *ms, *cs, inverse, down, bias, back_w)


def off_back_kernel(row_ref, key_ref, back_ref, a_ref, out_ref):
    step = pl.program_id(0)
    group = a_ref.shape[0]

    @pl.when(step == 0)
    def _():
        out_ref[...] = jnp.zeros_like(out_ref)

    for r in range(group):
        left = back_ref[:, lanes(row_ref[step * group + r])]
        out_ref[key_ref[0, step * group + r]] = dot(left, a_ref[r]).astype(BF)


def off_backward(row, key, back, off, slots_total):
    count, (cols, rows), group = off.shape[0], back.shape, 16
    return pl.pallas_call(
        off_back_kernel,
        grid_spec=pltpu.PrefetchScalarGridSpec(
            num_scalar_prefetch=2,
            grid=(count // group,),
            in_specs=[
                full((cols, rows)),
                pl.BlockSpec((group, BLK, BLK), lambda i, *_: (i, 0, 0)),
            ],
            out_specs=full((slots_total, cols, BLK)),
        ),
        out_shape=jax.ShapeDtypeStruct((slots_total, cols, BLK), BF),
        compiler_params=params(),
        name="off_backward",
    )(row, key, back, off)


def band_back_kernel(back_ref, self_ref, a_ref, out_ref, low_ref, high_ref, total):
    step = pl.program_id(0)
    group = a_ref.shape[0]
    cols, rows = self_ref.shape

    @pl.when(step == 0)
    def _():
        total[:, 0:BLK] = jnp.zeros((cols, BLK), F32)
        total[:, BLK : BLK + rows] = self_ref[...]
        total[:, BLK + rows :] = jnp.zeros((cols, BLK), F32)

    parts = []
    for r in range(group):
        left = back_ref[:, lanes(step * group + r)]
        right = jnp.concatenate([a_ref[r, 0], a_ref[r, 1], a_ref[r, 2]], axis=1)
        parts.append(dot(left, right))
    for c in range(group + 2):
        found = [
            parts[c - o][:, o * BLK : (o + 1) * BLK] for o in range(3) if 0 <= c - o < group
        ]
        at = lanes(step * group + c)
        total[:, at] = total[:, at] + sum(found[1:], found[0])

    @pl.when(step == pl.num_programs(0) - 1)
    def _():
        low_ref[...] = total[:, 0:BLK].astype(BF)
        out_ref[...] = total[:, BLK : BLK + rows]
        high_ref[...] = total[:, BLK + rows :].astype(BF)


def band_backward(back, self_part, band):
    cols, rows = back.shape
    blocks, group = band.shape[0], 8
    return pl.pallas_call(
        band_back_kernel,
        grid=(blocks // group,),
        in_specs=[
            full((cols, rows)),
            full((cols, rows)),
            pl.BlockSpec((group, 3, BLK, BLK), lambda i: (i, 0, 0, 0)),
        ],
        out_specs=[full((cols, rows)), full((cols, BLK)), full((cols, BLK))],
        out_shape=(
            jax.ShapeDtypeStruct((cols, rows), F32),
            jax.ShapeDtypeStruct((cols, BLK), BF),
            jax.ShapeDtypeStruct((cols, BLK), BF),
        ),
        scratch_shapes=[pltpu.VMEM((cols, rows + 2 * BLK), F32)],
        compiler_params=params(),
        cost_estimate=pl.CostEstimate(
            flops=2 * 32 * 3 * BLK * rows, bytes_accessed=9 * 1024 * 1024, transcendentals=0
        ),
        name="band_backward",
    )(back, self_part, band)


def collect_kernel(asked_ref, band_ref, low_ref, high_ref, in_ref, out_ref, total, table, sem):
    copy = pltpu.make_async_copy(asked_ref.at[:, 0, :], table, sem)
    copy.start()
    rows = band_ref.shape[1]
    total[...] = band_ref[...]
    total[:, 0:BLK] += low_ref[...].astype(F32)
    total[:, rows - BLK :] += high_ref[...].astype(F32)
    copy.wait()

    def body(p, carry):
        for s in range(CAP):
            at = lanes(table[p, s])
            total[:, at] = total[:, at] + in_ref[p, s].astype(F32)
        return carry

    lax.fori_loop(0, in_ref.shape[0], body, 0, unroll=4)
    out_ref[...] = total[...].astype(BF)


def collect(asked, band_sum, low, high, incoming):
    loop_size = asked.shape[0]
    vmem = pl.BlockSpec(memory_space=pltpu.VMEM)
    return pl.pallas_call(
        collect_kernel,
        in_specs=[pl.BlockSpec(memory_space=pl.ANY)] + [vmem] * 4,
        out_shape=jax.ShapeDtypeStruct(band_sum.shape, BF),
        scratch_shapes=[
            pltpu.VMEM(band_sum.shape, F32),
            pltpu.SMEM((loop_size, BLK), jnp.int32),
            pltpu.SemaphoreType.DMA,
        ],
        compiler_params=params(),
        name="collect",
    )(asked, band_sum, low, high, incoming)


def tile_sum_kernel(scale, in_ref, out_ref):
    total = jnp.sum(in_ref[...], axis=0) * scale
    for p in range(out_ref.shape[0]):
        out_ref[p] = total


def tile_sum(tiles, scale):
    return pl.pallas_call(
        lambda a, b: tile_sum_kernel(scale, a, b),
        out_shape=jax.ShapeDtypeStruct(tiles.shape, F32),
        name="tile_sum",
    )(tiles)


def tiles_kernel(in_ref, out_ref, bias_ref):
    groups = out_ref.shape[0] // 8
    for r in range(groups):
        for h in range(2):
            out_ref[8 * r : 8 * r + 8, h * BLK : (h + 1) * BLK] = in_ref[2 * r + h]
    bias_ref[...] = in_ref[2 * groups][0:1, 0 : bias_ref.shape[1]]


def tiles_apart(tiles, rows, hidden, part):
    return pl.pallas_call(
        tiles_kernel,
        out_shape=(
            jax.ShapeDtypeStruct((rows, hidden), F32),
            jax.ShapeDtypeStruct((1, part), F32),
        ),
        name="tiles_apart",
    )(tiles)


def per_device(
    features, band_blocks, off_blocks, off_row, off_col, off_part, w_self, w_neigh, bias, cotangent
):
    rows, cols = features.shape
    loop_size = lax.axis_size("loop")
    forward = [(i, (i + 1) % loop_size) for i in range(loop_size)]
    backward = [(b, a) for a, b in forward]
    swap = lambda x, k: lax.ppermute(x, "feat", [(i, i ^ k) for i in range(4)])
    spread = lambda x: lax.all_to_all(x, "loop", split_axis=0, concat_axis=0, tiled=True)

    def everywhere(x):
        far = swap(x, 2)
        return [x, swap(x, 1), far, swap(far, 1)]

    feat = lax.axis_index("feat").astype(jnp.int32).reshape(1)
    x, cot = features.T, cotangent.T
    key, request = slots(off_part.reshape(1, -1), off_col.reshape(1, -1), loop_size)
    asked = spread(request)

    pack = jnp.concatenate(
        [
            w_self.astype(F32),
            w_neigh.astype(F32),
            jnp.pad(bias.reshape(1, -1), ((0, 7), (0, w_self.shape[1] - bias.shape[0]))),
        ],
        axis=0,
    )
    down, bias_down, back_w = weights(feat, everywhere(pack))
    xs = everywhere(x)
    cs = everywhere(cot)

    low = lax.ppermute(x[:, rows - BLK :], "loop", forward)
    high = lax.ppermute(x[:, :BLK], "loop", backward)
    band_sum = band_forward(x, low, high, band_blocks)
    panels = spread(answers(asked, x))
    mean, inverse = off_forward(
        off_row, key, band_sum, panels.reshape(loop_size * CAP, cols, BLK), off_blocks
    )
    ms = everywhere(mean)
    hidden, back, self_part, tiles = dense(
        feat, xs, ms, cs, inverse, down, bias_down, back_w, loop_size
    )
    outgoing = off_backward(off_row, key, back, off_blocks, loop_size * CAP)
    incoming = spread(outgoing.reshape(loop_size, CAP, cols, BLK))
    back_sum, to_low, to_high = band_backward(back, self_part, band_blocks)
    from_low = lax.ppermute(to_high, "loop", forward)
    from_high = lax.ppermute(to_low, "loop", backward)

    sums = tile_sum(spread(tiles), 1.0 / math.sqrt(rows * loop_size))
    weight_grads, bias_grad = tiles_apart(
        spread(sums), 2 * cols, w_self.shape[1], bias.shape[0]
    )
    grad = collect(asked, back_sum, from_low, from_high, incoming)
    return (
        hidden.T,
        grad.T,
        weight_grads.reshape(2, cols, w_self.shape[1]),
        bias_grad.reshape(-1),
    )


def solution(mesh):
    return jax.shard_map(
        per_device,
        mesh=mesh,
        in_specs=(
            P("loop", "feat"),
            P("loop", None, None, None),
            P("loop", None, None),
            P("loop"),
            P("loop"),
            P("loop", None),
            P("feat", None),
            P("feat", None),
            P("feat"),
            P("loop", "feat"),
        ),
        out_specs=(P("loop", "feat"), P("loop", "feat"), P(None, "feat", None), P("feat")),
        check_vma=False,
    )
```

```python
import math

import jax
import jax.numpy as jnp
from jax import lax
from jax.experimental import pallas as pl
from jax.experimental.pallas import tpu as pltpu
from jax.sharding import PartitionSpec as P

BF = jnp.bfloat16
F32 = jnp.float32
I32 = jnp.int32
BLK = 128
ONES = 16
CAP = 4
SLOTS = CAP + 1
NN = (((1,), (0,)), ((), ()))
NT = (((1,), (1,)), ((), ()))
TT = (((0,), (1,)), ((), ()))
DMA = pltpu.SemaphoreType.DMA


def lanes(block, width=BLK):
    return pl.ds(pl.multiple_of(block * BLK, BLK), width)


def dot(a, b, dims=NN):
    return lax.dot_general(a, b, dims, preferred_element_type=F32)


def call(kernel, name, places, operands, results, scratch=(), aliases=None, flops=0, mib=16):
    spaces = {"v": pltpu.VMEM, "h": pltpu.HBM, "s": pltpu.SMEM, "a": pl.ANY, "w": pltpu.VMEM}
    ins, outs = places.split(">")
    held = [
        pltpu.with_memory_space_constraint(x, spaces[p]) if p in "vh" else x
        for p, x in zip(ins, operands, strict=True)
    ]
    nbytes = sum(math.prod(x.shape) * x.dtype.itemsize for x in operands)
    kinds = [
        pltpu.VMEM(shape, dtype) if p == "v" else jax.ShapeDtypeStruct(shape, dtype)
        for p, (shape, dtype) in zip(outs, results, strict=True)
    ]
    return pl.pallas_call(
        kernel,
        in_specs=[pl.BlockSpec(memory_space=spaces[p]) for p in ins],
        out_specs=[pl.BlockSpec(memory_space=spaces[p]) for p in outs],
        out_shape=kinds,
        scratch_shapes=list(scratch),
        input_output_aliases=aliases or {},
        compiler_params=pltpu.CompilerParams(vmem_limit_bytes=mib << 20),
        cost_estimate=pl.CostEstimate(flops=1, bytes_accessed=1, transcendentals=0),
        name=name,
    )(*held)


def near_rows(feat, k, rows):
    return pl.ds(pl.multiple_of(jnp.bitwise_xor(feat, k) * rows, BLK), rows)


def near_loop(me, shift, count):
    return lax.rem(me + shift + count, count)


def prepare_kernel(part_in, col_in, key_ref, request_ref, part_ref, col_ref, sems):
    copies = [
        pltpu.make_async_copy(part_in, part_ref, sems.at[0]),
        pltpu.make_async_copy(col_in, col_ref, sems.at[1]),
    ]
    for copy in copies:
        copy.start()
    for copy in copies:
        copy.wait()
    part, col = part_ref[...], col_ref[...]
    count = part.shape[1]
    first = lax.broadcasted_iota(I32, (count, count), 0)
    second = lax.broadcasted_iota(I32, (count, count), 1)
    part_down = jnp.sum(jnp.where(first == second, part, 0), axis=1, keepdims=True)
    earlier = (part_down == part) & (first < second)
    slot = jnp.sum(earlier.astype(I32), axis=0, keepdims=True)
    key_ref[...] = part * CAP + slot
    shape = request_ref.shape
    wide = (shape[0], shape[1], count)
    owner = lax.broadcasted_iota(I32, wide, 0)
    lane = lax.broadcasted_iota(I32, shape, 2)
    hit = owner == part[None]
    table = jnp.zeros(shape, I32)
    for s in range(CAP):
        value = jnp.sum(
            jnp.where(hit & (slot[None] == s), col[None], 0), axis=2, keepdims=True
        )
        table = jnp.where(lane == s, value, table)
    request_ref[...] = table


def prepare(part, col, loop_size):
    return call(
        prepare_kernel,
        "prepare",
        "hh>ww",
        (part, col),
        ((part.shape, I32), ((loop_size, 1, BLK), I32)),
        scratch=[pltpu.VMEM(part.shape, I32), pltpu.VMEM(col.shape, I32), DMA((2,))],
    )


def band_kernel(
    tie_ref, a_ref, off_ref, x_in, out_ref, off_held,
    band_ref, wide, total, sems, out_sems, more, x_sem,
):
    del tie_ref
    cols, rows = x_in.shape
    steps = sems.shape[0]
    group = a_ref.shape[0] // steps

    def copy(i):
        at = pl.ds(i * group, group)
        return pltpu.make_async_copy(a_ref.at[at], band_ref.at[at], sems.at[i])

    def send(i):
        at = lanes(i * group, group * BLK)
        return pltpu.make_async_copy(total.at[:, at], out_ref.at[:, at], out_sems.at[i])

    x_copy = pltpu.make_async_copy(x_in, wide.at[0:cols, BLK : BLK + rows], x_sem)
    x_copy.start()
    for i in range(steps):
        copy(i).start()
    late = pltpu.make_async_copy(off_ref, off_held, more)
    late.start()
    wide[0:cols, 0:BLK] = jnp.zeros((cols, BLK), BF)
    wide[0:cols, BLK + rows :] = jnp.zeros((cols, BLK), BF)
    wide[cols:, :] = jnp.ones((ONES, wide.shape[1]), BF)
    x_copy.wait()

    def body(i, carry):
        copy(i).wait()
        for r in range(group):
            b = i * group + r
            left = wide[:, lanes(b, 3 * BLK)]
            right = jnp.concatenate([band_ref[b, 0], band_ref[b, 1], band_ref[b, 2]], axis=1)
            total[:, lanes(b)] = dot(left, right, NT)
        send(i).start()
        return carry

    lax.fori_loop(0, steps, body, 0)
    for i in range(steps):
        send(i).wait()
    late.wait()


def band_forward(tie, band, off, x):
    cols, rows = x.shape
    return call(
        band_kernel,
        "band_forward",
        "shhh>hv",
        (tie, band, off, x),
        (((cols + ONES, rows), F32), (off.shape, BF)),
        scratch=[
            pltpu.VMEM(band.shape, BF),
            pltpu.VMEM((cols + ONES, rows + 2 * BLK), BF),
            pltpu.VMEM((cols + ONES, rows), F32),
            DMA((8,)),
            DMA((8,)),
            DMA,
            DMA,
        ],
        flops=2 * (cols + ONES) * 3 * BLK * rows,
    )


def pieces_kernel(
    place_ref, x_ref, cot_ref, self_in, neigh_in, bias_in, p0, p1, p2, p3,
    held, self_ref, neigh_ref, bias_ref, sems, out_sems, more,
):
    cols, part = x_ref.shape[0], cot_ref.shape[0]
    tall = cols + part
    copies, sends = [], []
    for k, piece in enumerate((p0, p1, p2, p3)):
        at = near_rows(place_ref[0], k, piece.shape[1])
        copies.append(
            pltpu.make_async_copy(x_ref.at[:, at], held.at[k, 0:cols], sems.at[2 * k])
        )
        copies.append(
            pltpu.make_async_copy(cot_ref.at[:, at], held.at[k, cols:tall], sems.at[2 * k + 1])
        )
        sends.append(pltpu.make_async_copy(held.at[k], piece, out_sems.at[k]))
    small = [
        pltpu.make_async_copy(a, b, more.at[i])
        for i, (a, b) in enumerate(
            ((self_in, self_ref), (neigh_in, neigh_ref), (bias_in, bias_ref))
        )
    ]
    for copy in small:
        copy.start()
    for k in (1, 2, 3, 0):
        copies[2 * k].start()
        copies[2 * k + 1].start()
    for copy in small:
        copy.wait()
    hidden = self_ref.shape[1]
    bias = bias_ref[...]
    high = bias.astype(BF)
    rest = bias - high.astype(F32)
    middle = rest.astype(BF)
    low = (rest - middle.astype(F32)).astype(BF)
    row = lax.broadcasted_iota(I32, (16, part), 0)
    lines = [jnp.broadcast_to(v.astype(F32), (16, part)) for v in (high, middle, low)]
    lines = jnp.where(row == 0, lines[0], jnp.where(row == 1, lines[1], lines[2]))
    lines = jnp.where(row < 3, lines, 0.0).astype(BF)
    for k in range(4):
        held[k, tall:, :] = jnp.zeros((16, held.shape[2]), BF)
        for g in range(cols // 16):
            rows = slice(16 * g, 16 * g + 16)
            held[k, tall:, 2 * g * hidden : (2 * g + 1) * hidden] = self_ref[rows, :]
            held[k, tall:, (2 * g + 1) * hidden : (2 * g + 2) * hidden] = neigh_ref[rows, :]
        held[k, tall:, cols // 8 * hidden : cols // 8 * hidden + part] = lines
    for k in (1, 2, 3, 0):
        copies[2 * k].wait()
        copies[2 * k + 1].wait()
        sends[k].start()
    for send in sends:
        send.wait()


def by_device(place, x, cot, w_self, w_neigh, bias):
    piece = (x.shape[0] + cot.shape[0] + 16, x.shape[1] // 4)
    return call(
        pieces_kernel,
        "by_device",
        "shhhhh>hhhh",
        (place, x, cot, w_self, w_neigh, bias),
        4 * ((piece, BF),),
        scratch=[
            pltpu.VMEM((4, *piece), BF),
            pltpu.VMEM(w_self.shape, BF),
            pltpu.VMEM(w_neigh.shape, BF),
            pltpu.VMEM(bias.shape, F32),
            DMA((8,)),
            DMA((4,)),
            DMA((3,)),
        ],
    )


def answer_kernel(place_ref, asked_ref, x_in, out_ref, x_ref, held, table, sem, x_sem, sems):
    copy = pltpu.make_async_copy(asked_ref.at[:, 0, :], table, sem)
    x_copy = pltpu.make_async_copy(x_in, x_ref, x_sem)
    copy.start()
    x_copy.start()
    count, steps = held.shape[0], sems.shape[0]
    group = count // steps
    above = near_loop(place_ref[1], 1, count)

    def send(j):
        at = pl.ds(j * group, group)
        return pltpu.make_async_copy(held.at[at], out_ref.at[at], sems.at[j])

    def body(p, carry):
        for s in range(CAP):
            held[p, s] = x_ref[:, lanes(table[p, s])]
        edge = jnp.where(p == above, x_ref.shape[1] // BLK - 1, 0)
        held[p, CAP] = x_ref[:, lanes(edge)]
        return carry

    copy.wait()
    x_copy.wait()
    for j in range(steps):
        lax.fori_loop(j * group, (j + 1) * group, body, 0, unroll=4)
        send(j).start()
    for j in range(steps):
        send(j).wait()


def answers(place, asked, x):
    shape = (asked.shape[0], SLOTS, x.shape[0], BLK)
    (out,) = call(
        answer_kernel,
        "answers",
        "sah>h",
        (place, asked, x),
        ((shape, BF),),
        scratch=[
            pltpu.VMEM(x.shape, BF),
            pltpu.VMEM(shape, BF),
            pltpu.SMEM((shape[0], BLK), I32),
            DMA,
            DMA,
            DMA((4,)),
        ],
    )
    return out


def off_kernel(
    place_ref, row_ref, key_ref, start_in, band_in, panel_in, a_ref,
    m0, m1, m2, m3, inverse_ref, total, edge_ref, panel_ref, sems,
):
    feat = place_ref[0]
    cols, rows = m0.shape[0], total.shape[1]
    count = a_ref.shape[0]
    pairs = [
        (panel_in, panel_ref), (start_in, total),
        (band_in.at[0, 0], edge_ref.at[0]), (band_in.at[band_in.shape[0] - 1, 2], edge_ref.at[1]),
    ]
    copies = [pltpu.make_async_copy(a, b, sems.at[i]) for i, (a, b) in enumerate(pairs)]
    for copy in copies:
        copy.start()
    for copy in copies:
        copy.wait()
    below, above = [near_loop(place_ref[1], d, panel_ref.shape[0]) for d in (-1, 1)]
    total[0:cols, 0:BLK] += dot(panel_ref[below, CAP], edge_ref[0], NT)
    total[0:cols, rows - BLK :] += dot(panel_ref[above, CAP], edge_ref[1], NT)
    ones = jnp.ones((ONES, BLK), BF)
    for start in range(0, count, 8):
        terms = []
        for r in range(start, start + 8):
            key = key_ref[0, r]
            left = jnp.concatenate([panel_ref[key // CAP, key % CAP], ones], axis=0)
            terms.append(dot(left, a_ref[r], NT))
        for r in range(start, start + 8):
            where = lanes(row_ref[r])
            total[:, where] = total[:, where] + terms[r - start]
    part = m0.shape[1]
    for k, mean_ref in enumerate((m1, m2, m3, m0)):
        at = near_rows(feat, (k + 1) % 4, part)
        inverse = 1.0 / (1.0 + total[cols : cols + 1, at])
        mean_ref[...] = (total[0:cols, at] * inverse).astype(BF)
        if k == 3:
            inverse_ref[...] = inverse


def off_forward(place, row, key, band_sum, band, panels, off):
    cols, rows = panels.shape[2], band_sum.shape[1]
    mean = ((cols, rows // 4), BF)
    return call(
        off_kernel,
        "off_forward",
        "ssshhhv>vvvvv",
        (place, row, key, band_sum, band, panels, off),
        4 * (mean,) + (((1, rows // 4), F32),),
        scratch=[
            pltpu.VMEM(band_sum.shape, F32),
            pltpu.VMEM((2, BLK, BLK), BF),
            pltpu.VMEM(panels.shape, BF),
            DMA((4,)),
        ],
        flops=2 * off.shape[0] * BLK * BLK * (cols + ONES),
    )


def weights_kernel(place_ref, p0, p1, p2, p3, down_ref, bias_ref, back_ref):
    feat = place_ref[0]
    hidden = down_ref.shape[0]
    cols, part = back_ref.shape[0] // 8, hidden // 4
    here = lax.broadcasted_iota(I32, (hidden, hidden), 0)
    there = lax.broadcasted_iota(I32, (hidden, hidden), 1)
    place = (jnp.bitwise_xor(there // part, feat)) * part + there % part
    chosen = jnp.where(here == place, 0.5, 0.0).astype(BF)
    eye = lax.broadcasted_iota(I32, (part, part), 0) == lax.broadcasted_iota(
        I32, (part, part), 1
    )
    own, neigh = [], []
    for k, p in enumerate((p0, p1, p2, p3)):
        rows = slice(cols + part, cols + part + 16)
        for g in range(cols // 16):
            own.append(p[rows, 2 * g * hidden : (2 * g + 1) * hidden])
            neigh.append(p[rows, (2 * g + 1) * hidden : (2 * g + 2) * hidden])
        start = cols // 8 * hidden
        lines = p[rows, start : start + BLK].astype(F32)[:, 0:part]
        line = (lines[0:1] + lines[1:2]) + lines[2:3]
        bias_ref[k * part : (k + 1) * part, :] = 0.5 * jnp.sum(
            jnp.where(eye, line, 0.0), axis=1, keepdims=True
        )
    down_ref[...] = dot(chosen, jnp.concatenate(own + neigh, axis=0), TT).astype(BF)
    back_ref[...] = dot(jnp.concatenate(neigh + own, axis=0), chosen).astype(BF)


def weights(place, pieces, cols, hidden):
    return call(
        weights_kernel,
        "weights",
        "svvvv>vvv",
        (place, *pieces),
        (((hidden, 8 * cols), BF), ((hidden, 1), F32), ((8 * cols, hidden), BF)),
    )


def dense_kernel(
    p0, p1, p2, p3, m0, m1, m2, m3, inverse_ref, down_ref, bias_ref, back_w_ref,
    b0, b1, b2, b3, grad_ref, h0, h1, h2, h3, helds, sems,
):
    cols, rows = m0.shape
    pieces = (p0, p1, p2, p3)
    part = h0.shape[0] - cols
    width = 2 * BLK

    def project(i):
        at = slice(i * width, (i + 1) * width)
        both = [p[0:cols, at] for p in pieces] + [m[:, at] for m in (m0, m1, m2, m3)]
        return dot(down_ref[...], jnp.concatenate(both, axis=0))

    def gradient(i, half):
        at = slice(i * width, (i + 1) * width)
        grads = []
        for k, p in enumerate(pieces):
            here = slice(k * part, (k + 1) * part)
            u = half[here] + bias_ref[here]
            t = jnp.tanh(u)
            s = 1.0 + t
            helds[k, 0:part, at] = (u * s).astype(BF)
            c = p[cols : cols + part, at].astype(F32)
            grads.append((c * s * (1.0 + u * (1.0 - t))).astype(BF))
        return jnp.concatenate(grads, axis=0)

    def products(i, grad):
        at = slice(i * width, (i + 1) * width)
        grad_ref[:, at] = grad
        both = dot(back_w_ref[...], grad)
        backs = both[0 : 4 * cols] * inverse_ref[:, at]
        for k, b in enumerate((b0, b1, b2, b3)):
            b[:, at] = backs[k * cols : (k + 1) * cols].astype(BF)
            own = both[(4 + k) * cols : (5 + k) * cols]
            helds[k, part:, at] = own.astype(BF)

    count = rows // width
    half, grad = project(0), None
    for i in range(count):
        later = project(i + 1) if i + 1 < count else None
        fresh = gradient(i, half)
        if grad is not None:
            products(i - 1, grad)
        half, grad = later, fresh
    products(count - 1, grad)
    sends = []
    for k, h in enumerate((h0, h1, h2, h3)):
        sends.append(pltpu.make_async_copy(helds.at[k], h, sems.at[k]))
        sends[-1].start()
    for send in sends:
        send.wait()


def dense(pieces, ms, inverse, down, bias, back_w):
    cols, rows = ms[0].shape
    hidden = down.shape[0]
    return call(
        dense_kernel,
        "dense",
        12 * "v" + ">vvvvvhhhh",
        (*pieces, *ms, inverse, down, bias, back_w),
        4 * (((cols, rows), BF),)
        + (((hidden, rows), BF),)
        + 4 * (((hidden // 4 + cols, rows), BF),),
        scratch=[pltpu.VMEM((4, hidden // 4 + cols, rows), BF), DMA((4,))],
        flops=2 * rows * hidden * 400,
    )


def after_kernel(feat_ref, p0, p1, p2, p3, m0, m1, m2, m3, grad_ref, g0, g1, g2, g3):
    cols, rows = m0.shape
    part = grad_ref.shape[0] // 4
    grad = grad_ref[...]
    left = [p[0:cols, :] for p in (p0, p1, p2, p3)] + [m[...] for m in (m0, m1, m2, m3)]
    left.append(jnp.ones((ONES, rows), BF))
    total = dot(jnp.concatenate(left, axis=0), grad, NT)
    feat = feat_ref[0]
    low, high = total[:, 0:BLK], total[:, BLK:]
    far = (feat & 2) != 0
    halves = [jnp.where(far, high, low), jnp.where(far, low, high)]
    halves = [jnp.where((feat & 1) != 0, pltpu.roll(h, part, 1), h) for h in halves]
    tall = 4 * cols
    for k, out in enumerate((g0, g1, g2, g3)):
        for h in range(2):
            at = slice(h * BLK, (h + 1) * BLK)
            out[0:cols, at] = halves[h][k * cols : (k + 1) * cols]
            out[cols : 2 * cols, at] = halves[h][tall + k * cols : tall + (k + 1) * cols]
        line = (low if k < 2 else high)[2 * tall : 2 * tall + 8]
        out[2 * cols :, 0:BLK] = pltpu.roll(line, part, 1) if k % 2 else line
        out[2 * cols :, BLK:] = jnp.zeros((8, BLK), F32)


def after(place, pieces, ms, grad):
    cols, _ = ms[0].shape
    return call(
        after_kernel,
        "after",
        "s" + 9 * "v" + ">wwww",
        (place, *pieces, *ms, grad),
        4 * (((2 * cols + 8, grad.shape[0]), F32),),
    )


def off_back_kernel(
    place_ref, row_ref, key_ref, b0, b1, b2, b3, a_ref, band_ref, out_ref, back_ref,
    held, edge_ref, sem, sems,
):
    count = band_ref.shape[0]
    edges = [
        pltpu.make_async_copy(band_ref.at[0, 0], edge_ref.at[0], sems.at[0]),
        pltpu.make_async_copy(band_ref.at[count - 1, 2], edge_ref.at[1], sems.at[1]),
    ]
    for edge in edges:
        edge.start()
    for k, b in enumerate((b0, b1, b2, b3)):
        back_ref[:, near_rows(place_ref[0], k, b.shape[1])] = b[...]
    held[...] = jnp.zeros_like(held)
    for r in range(a_ref.shape[0]):
        key = key_ref[0, r]
        left = back_ref[:, lanes(row_ref[r])]
        held[key // CAP, key % CAP] = dot(left, a_ref[r]).astype(BF)
    for edge in edges:
        edge.wait()
    below, above = [near_loop(place_ref[1], d, held.shape[0]) for d in (-1, 1)]
    rows = back_ref.shape[1]
    held[below, CAP] = dot(back_ref[:, 0:BLK], edge_ref[0]).astype(BF)
    held[above, CAP] = dot(back_ref[:, rows - BLK :], edge_ref[1]).astype(BF)
    copy = pltpu.make_async_copy(held, out_ref, sem)
    copy.start()
    copy.wait()


def off_backward(place, row, key, backs, off, band, loop_size):
    cols, part = backs[0].shape
    shape = (loop_size, SLOTS, cols, BLK)
    return call(
        off_back_kernel,
        "off_backward",
        "sssvvvvvh>hv",
        (place, row, key, *backs, off, band),
        ((shape, BF), ((cols, 4 * part), BF)),
        scratch=[pltpu.VMEM(shape, BF), pltpu.VMEM((2, BLK, BLK), BF), DMA, DMA((2,))],
    )


def band_back_kernel(back_ref, a_ref, total, held, sems):
    count, steps = a_ref.shape[0], sems.shape[0]
    group = count // steps
    copies = []
    for i in range(steps):
        at = pl.ds(i * group, group)
        copies.append(pltpu.make_async_copy(a_ref.at[at], held.at[at], sems.at[i]))
        copies[-1].start()
    carried = [None, None]
    for i in range(steps):
        copies[i].wait()
        for b in range(i * group, (i + 1) * group):
            right = jnp.concatenate([held[b, 0], held[b, 1], held[b, 2]], axis=1)
            term = dot(back_ref[:, b * BLK : (b + 1) * BLK], right)
            first, middle, last = [term[:, o * BLK : (o + 1) * BLK] for o in range(3)]
            if b > 0:
                total[:, (b - 1) * BLK : b * BLK] = carried[0] + first
            carried = [middle if b == 0 else carried[1] + middle, last]
    total[:, (count - 1) * BLK :] = carried[0]


def band_backward(back, band):
    cols, rows = back.shape
    (out,) = call(
        band_back_kernel,
        "band_backward",
        "vh>w",
        (back, band),
        (((cols, rows), F32),),
        scratch=[pltpu.VMEM(band.shape, BF), DMA((8,))],
    )
    return out


def collect_kernel(
    place_ref, asked_ref, start_ref, in_ref, h0, h1, h2, h3,
    out_ref, hidden_ref, total, held, selfs, table, sems,
):
    feat = place_ref[0]
    (cols, rows), part = total.shape, h0.shape[1]
    hidden = h0.shape[0] - cols
    copies = [
        pltpu.make_async_copy(asked_ref.at[:, 0, :], table, sems.at[0]),
        pltpu.make_async_copy(start_ref, total, sems.at[1]),
        pltpu.make_async_copy(in_ref, held, sems.at[2]),
    ]
    for k, h in enumerate((h0, h1, h2, h3)):
        copies.append(pltpu.make_async_copy(h.at[hidden:], selfs.at[k], sems.at[3 + k]))
    for k, h in enumerate((h0, h1, h2, h3)):
        at = near_rows(feat, k, part)
        copies.append(
            pltpu.make_async_copy(h.at[0:hidden], hidden_ref.at[:, at], sems.at[7 + k])
        )
    for copy in copies:
        copy.start()
    copies[1].wait()
    for k in range(4):
        copies[3 + k].wait()
        at = near_rows(feat, k, part)
        total[:, at] = total[:, at] + selfs[k].astype(F32)
    copies[0].wait()
    copies[2].wait()
    below, above = [near_loop(place_ref[1], d, held.shape[0]) for d in (-1, 1)]
    total[:, 0:BLK] += held[below, CAP].astype(F32)
    total[:, rows - BLK :] += held[above, CAP].astype(F32)

    def body(p, carry):
        for s in range(CAP):
            at = lanes(table[p, s])
            total[:, at] = total[:, at] + held[p, s].astype(F32)
        return carry

    lax.fori_loop(0, held.shape[0], body, 0, unroll=4)
    out_ref[...] = total[...].astype(BF)
    for copy in copies[7:]:
        copy.wait()


def collect(place, asked, band_sum, incoming, outs):
    cols, rows = band_sum.shape
    return call(
        collect_kernel,
        "collect",
        "saah" + 4 * "h" + ">ww",
        (place, asked, band_sum, incoming, *outs),
        ((band_sum.shape, BF), ((outs[0].shape[0] - cols, rows), BF)),
        scratch=[
            pltpu.VMEM(band_sum.shape, F32),
            pltpu.VMEM(incoming.shape, BF),
            pltpu.VMEM((4, cols, rows // 4), BF),
            pltpu.SMEM((asked.shape[0], BLK), I32),
            DMA((11,)),
        ],
    )


def finish_kernel(scale, own_ref, other_ref, out_ref, bias_ref):
    total = (own_ref[...] + other_ref[...]) * scale
    tall = out_ref.shape[0]
    out_ref[...] = total[0:tall]
    bias_ref[...] = total[tall : tall + 1, 0 : bias_ref.shape[1]]


def finish(own, other, part, scale):
    tall, wide = own.shape
    return call(
        lambda *refs: finish_kernel(scale, *refs),
        "finish",
        "ww>ww",
        (own, other),
        (((tall - 8, wide), F32), ((1, part), F32)),
    )


def per_device(
    features, band_blocks, off_blocks, off_row, off_col, off_part, w_self, w_neigh, bias, cotangent
):
    rows, cols = features.shape
    loop_size = lax.axis_size("loop")
    together = lax.optimization_barrier

    def swap(value, k, j=0):
        pairs = [(4 * i + f, 4 * (i ^ j) + (f ^ k)) for i in range(loop_size) for f in range(4)]
        return lax.ppermute(value, ("loop", "feat"), pairs)

    def swapped(values):
        return [values[0]] + [swap(values[k], k) for k in (1, 2, 3)]

    def spread(value):
        return lax.all_to_all(value, "loop", split_axis=0, concat_axis=0, tiled=True)

    place = jnp.stack([lax.axis_index("feat"), lax.axis_index("loop")]).astype(I32)
    x, cot = features.T, cotangent.T
    key, request = prepare(off_part.reshape(1, -1), off_col.reshape(1, -1), loop_size)
    request, place = together((request, place))
    asked = spread(request)
    pieces = by_device(place, x, cot, w_self, w_neigh, bias.reshape(1, -1))
    asked, then = together((asked, pieces[0]))[0], place
    pieces = swapped(pieces)
    ready = answers(place, asked, x)
    ready, then = together((ready, then))
    panels = spread(ready)
    band_sum, off = band_forward(then, band_blocks, off_blocks, x)
    *ms, inverse = off_forward(place, off_row, key, band_sum, band_blocks, panels, off)
    ms = swapped(ms)
    down, bias_down, back_w = weights(place, pieces, cols, w_self.shape[1])
    ms, down = together((ms, down))
    *rest, h0, h1, h2, h3 = dense(pieces, ms, inverse, down, bias_down, back_w)
    *backs, grad = rest
    backs = swapped(backs)
    terms = after(place, pieces, ms, grad)
    near = swapped(terms)
    o2 = swap(h2, 2)
    backs, h1, h3 = together((backs, h1, h3))
    outgoing, back = off_backward(place, off_row, key, backs, off, band_blocks, loop_size)
    grads = (near[0] + near[1]) + (near[2] + near[3])
    one, two, three = [swap(grads, 0, j) for j in (8, 16, 24)]
    outgoing, back, one, two, three, o2, h1, h3 = together(
        (outgoing, back, one, two, three, o2, h1, h3)
    )
    incoming = spread(outgoing)
    outs = [h0, swap(h1, 1), o2, swap(h3, 3)]
    back_sum = band_backward(back, band_blocks)
    one, two, three, back_sum = together((one, two, three, back_sum))
    grads = (grads + one) + (two + three)
    one, two, three = [swap(grads, 0, j) for j in (2, 4, 6)]
    grads = (grads + one) + (two + three)
    other = swap(grads, 0, 1)
    grad_features, hidden = collect(place, asked, back_sum, incoming, outs)
    weight_grads, bias_grad = finish(
        grads, other, bias.shape[0], 0.5 / math.sqrt(rows * loop_size)
    )
    return (
        hidden.T,
        grad_features.T,
        weight_grads.reshape(2, cols, w_self.shape[1]),
        bias_grad.reshape(-1),
    )


def solution(mesh):
    return jax.shard_map(
        per_device,
        mesh=mesh,
        in_specs=(
            P("loop", "feat"),
            P("loop", None, None, None),
            P("loop", None, None),
            P("loop"),
            P("loop"),
            P("loop", None),
            P("feat", None),
            P("feat", None),
            P("feat"),
            P("loop", "feat"),
        ),
        out_specs=(P("loop", "feat"), P("loop", "feat"), P(None, "feat", None), P("feat")),
        check_vma=False,
    )
```

```python
import math

import jax
import jax.numpy as jnp
from jax import lax
from jax.experimental import pallas as pl
from jax.experimental.pallas import tpu as pltpu
from jax.sharding import PartitionSpec as P

BF = jnp.bfloat16
F32 = jnp.float32
I32 = jnp.int32
BLK = 128
ONES = 16
CAP = 4
SLOTS = CAP + 1
NN = (((1,), (0,)), ((), ()))
NT = (((1,), (1,)), ((), ()))
TT = (((0,), (1,)), ((), ()))
DMA = pltpu.SemaphoreType.DMA


def lanes(block, width=BLK):
    return pl.ds(pl.multiple_of(block * BLK, BLK), width)


def dot(a, b, dims=NN):
    return lax.dot_general(a, b, dims, preferred_element_type=F32)


def call(kernel, name, places, operands, results, scratch=(), aliases=None, flops=0, mib=16):
    spaces = {"v": pltpu.VMEM, "h": pltpu.HBM, "s": pltpu.SMEM, "a": pl.ANY, "w": pltpu.VMEM}
    ins, outs = places.split(">")
    held = [
        pltpu.with_memory_space_constraint(x, spaces[p]) if p in "vh" else x
        for p, x in zip(ins, operands, strict=True)
    ]
    nbytes = sum(math.prod(x.shape) * x.dtype.itemsize for x in operands)
    kinds = [
        pltpu.VMEM(shape, dtype) if p == "v" else jax.ShapeDtypeStruct(shape, dtype)
        for p, (shape, dtype) in zip(outs, results, strict=True)
    ]
    return pl.pallas_call(
        kernel,
        in_specs=[pl.BlockSpec(memory_space=spaces[p]) for p in ins],
        out_specs=[pl.BlockSpec(memory_space=spaces[p]) for p in outs],
        out_shape=kinds,
        scratch_shapes=list(scratch),
        input_output_aliases=aliases or {},
        compiler_params=pltpu.CompilerParams(vmem_limit_bytes=mib << 20),
        cost_estimate=pl.CostEstimate(flops=1, bytes_accessed=1, transcendentals=0),
        name=name,
    )(*held)


def near_rows(feat, k, rows):
    return pl.ds(pl.multiple_of(jnp.bitwise_xor(feat, k) * rows, BLK), rows)


def near_loop(me, shift, count):
    return lax.rem(me + shift + count, count)


def prepare_kernel(part_in, col_in, key_ref, request_ref, part_ref, col_ref, sems):
    copies = [
        pltpu.make_async_copy(part_in, part_ref, sems.at[0]),
        pltpu.make_async_copy(col_in, col_ref, sems.at[1]),
    ]
    for copy in copies:
        copy.start()
    for copy in copies:
        copy.wait()
    part, col = part_ref[...], col_ref[...]
    count = part.shape[1]
    first = lax.broadcasted_iota(I32, (count, count), 0)
    second = lax.broadcasted_iota(I32, (count, count), 1)
    part_down = jnp.sum(jnp.where(first == second, part, 0), axis=1, keepdims=True)
    earlier = (part_down == part) & (first < second)
    slot = jnp.sum(earlier.astype(I32), axis=0, keepdims=True)
    key_ref[...] = part * CAP + slot
    shape = request_ref.shape
    wide = (shape[0], shape[1], count)
    owner = lax.broadcasted_iota(I32, wide, 0)
    lane = lax.broadcasted_iota(I32, shape, 2)
    hit = owner == part[None]
    table = jnp.zeros(shape, I32)
    for s in range(CAP):
        value = jnp.sum(
            jnp.where(hit & (slot[None] == s), col[None], 0), axis=2, keepdims=True
        )
        table = jnp.where(lane == s, value, table)
    request_ref[...] = table


def prepare(part, col, loop_size):
    return call(
        prepare_kernel,
        "prepare",
        "hh>ww",
        (part, col),
        ((part.shape, I32), ((loop_size, 1, BLK), I32)),
        scratch=[pltpu.VMEM(part.shape, I32), pltpu.VMEM(col.shape, I32), DMA((2,))],
    )


def band_kernel(
    tie_ref, a_ref, off_ref, x_in, out_ref, off_held,
    band_ref, wide, total, sems, out_sems, more, x_sem,
):
    del tie_ref
    cols, rows = x_in.shape
    steps = sems.shape[0]
    group = a_ref.shape[0] // steps

    def copy(i):
        at = pl.ds(i * group, group)
        return pltpu.make_async_copy(a_ref.at[at], band_ref.at[at], sems.at[i])

    def send(i):
        at = lanes(i * group, group * BLK)
        return pltpu.make_async_copy(total.at[:, at], out_ref.at[:, at], out_sems.at[i])

    x_copy = pltpu.make_async_copy(x_in, wide.at[0:cols, BLK : BLK + rows], x_sem)
    x_copy.start()
    for i in range(steps):
        copy(i).start()
    late = pltpu.make_async_copy(off_ref, off_held, more)
    late.start()
    wide[0:cols, 0:BLK] = jnp.zeros((cols, BLK), BF)
    wide[0:cols, BLK + rows :] = jnp.zeros((cols, BLK), BF)
    wide[cols:, :] = jnp.ones((ONES, wide.shape[1]), BF)
    x_copy.wait()

    def body(i, carry):
        copy(i).wait()
        for r in range(group):
            b = i * group + r
            left = wide[:, lanes(b, 3 * BLK)]
            right = jnp.concatenate([band_ref[b, 0], band_ref[b, 1], band_ref[b, 2]], axis=1)
            total[:, lanes(b)] = dot(left, right, NT)
        send(i).start()
        return carry

    lax.fori_loop(0, steps, body, 0)
    for i in range(steps):
        send(i).wait()
    late.wait()


def band_forward(tie, band, off, x):
    cols, rows = x.shape
    return call(
        band_kernel,
        "band_forward",
        "shhh>hv",
        (tie, band, off, x),
        (((cols + ONES, rows), F32), (off.shape, BF)),
        scratch=[
            pltpu.VMEM(band.shape, BF),
            pltpu.VMEM((cols + ONES, rows + 2 * BLK), BF),
            pltpu.VMEM((cols + ONES, rows), F32),
            DMA((8,)),
            DMA((8,)),
            DMA,
            DMA,
        ],
        flops=2 * (cols + ONES) * 3 * BLK * rows,
    )


def pieces_kernel(
    place_ref, x_ref, cot_ref, self_in, neigh_in, bias_in, p0, p1, p2, p3,
    held, self_ref, neigh_ref, bias_ref, sems, out_sems, more,
):
    cols, part = x_ref.shape[0], cot_ref.shape[0]
    tall = cols + part
    copies, sends = [], []
    for k, piece in enumerate((p0, p1, p2, p3)):
        at = near_rows(place_ref[0], k, piece.shape[1])
        copies.append(
            pltpu.make_async_copy(x_ref.at[:, at], held.at[k, 0:cols], sems.at[2 * k])
        )
        copies.append(
            pltpu.make_async_copy(cot_ref.at[:, at], held.at[k, cols:tall], sems.at[2 * k + 1])
        )
        sends.append(pltpu.make_async_copy(held.at[k], piece, out_sems.at[k]))
    small = [
        pltpu.make_async_copy(a, b, more.at[i])
        for i, (a, b) in enumerate(
            ((self_in, self_ref), (neigh_in, neigh_ref), (bias_in, bias_ref))
        )
    ]
    for copy in small:
        copy.start()
    for k in (1, 2, 3, 0):
        copies[2 * k].start()
        copies[2 * k + 1].start()
    for copy in small:
        copy.wait()
    hidden = self_ref.shape[1]
    bias = bias_ref[...]
    high = bias.astype(BF)
    rest = bias - high.astype(F32)
    middle = rest.astype(BF)
    low = (rest - middle.astype(F32)).astype(BF)
    row = lax.broadcasted_iota(I32, (16, part), 0)
    lines = [jnp.broadcast_to(v.astype(F32), (16, part)) for v in (high, middle, low)]
    lines = jnp.where(row == 0, lines[0], jnp.where(row == 1, lines[1], lines[2]))
    lines = jnp.where(row < 3, lines, 0.0).astype(BF)
    for k in range(4):
        held[k, tall:, :] = jnp.zeros((16, held.shape[2]), BF)
        for g in range(cols // 16):
            rows = slice(16 * g, 16 * g + 16)
            held[k, tall:, 2 * g * hidden : (2 * g + 1) * hidden] = self_ref[rows, :]
            held[k, tall:, (2 * g + 1) * hidden : (2 * g + 2) * hidden] = neigh_ref[rows, :]
        held[k, tall:, cols // 8 * hidden : cols // 8 * hidden + part] = lines
    for k in (1, 2, 3, 0):
        copies[2 * k].wait()
        copies[2 * k + 1].wait()
        sends[k].start()
    for send in sends:
        send.wait()


def by_device(place, x, cot, w_self, w_neigh, bias):
    piece = (x.shape[0] + cot.shape[0] + 16, x.shape[1] // 4)
    return call(
        pieces_kernel,
        "by_device",
        "shhhhh>hhhh",
        (place, x, cot, w_self, w_neigh, bias),
        4 * ((piece, BF),),
        scratch=[
            pltpu.VMEM((4, *piece), BF),
            pltpu.VMEM(w_self.shape, BF),
            pltpu.VMEM(w_neigh.shape, BF),
            pltpu.VMEM(bias.shape, F32),
            DMA((8,)),
            DMA((4,)),
            DMA((3,)),
        ],
    )


def answer_kernel(place_ref, asked_ref, x_in, out_ref, x_ref, held, table, sem, x_sem, sems):
    copy = pltpu.make_async_copy(asked_ref.at[:, 0, :], table, sem)
    x_copy = pltpu.make_async_copy(x_in, x_ref, x_sem)
    copy.start()
    x_copy.start()
    count, steps = held.shape[0], sems.shape[0]
    group = count // steps
    above = near_loop(place_ref[1], 1, count)

    def send(j):
        at = pl.ds(j * group, group)
        return pltpu.make_async_copy(held.at[at], out_ref.at[at], sems.at[j])

    def body(p, carry):
        for s in range(CAP):
            held[p, s] = x_ref[:, lanes(table[p, s])]
        edge = jnp.where(p == above, x_ref.shape[1] // BLK - 1, 0)
        held[p, CAP] = x_ref[:, lanes(edge)]
        return carry

    copy.wait()
    x_copy.wait()
    for j in range(steps):
        lax.fori_loop(j * group, (j + 1) * group, body, 0, unroll=4)
        send(j).start()
    for j in range(steps):
        send(j).wait()


def answers(place, asked, x):
    shape = (asked.shape[0], SLOTS, x.shape[0], BLK)
    (out,) = call(
        answer_kernel,
        "answers",
        "sah>h",
        (place, asked, x),
        ((shape, BF),),
        scratch=[
            pltpu.VMEM(x.shape, BF),
            pltpu.VMEM(shape, BF),
            pltpu.SMEM((shape[0], BLK), I32),
            DMA,
            DMA,
            DMA((4,)),
        ],
    )
    return out


def off_kernel(
    place_ref, row_ref, key_ref, start_in, band_in, panel_in, a_ref,
    m0, m1, m2, m3, inverse_ref, total, edge_ref, panel_ref, sems,
):
    feat = place_ref[0]
    cols, rows = m0.shape[0], total.shape[1]
    count = a_ref.shape[0]
    pairs = [
        (panel_in, panel_ref), (start_in, total),
        (band_in.at[0, 0], edge_ref.at[0]), (band_in.at[band_in.shape[0] - 1, 2], edge_ref.at[1]),
    ]
    copies = [pltpu.make_async_copy(a, b, sems.at[i]) for i, (a, b) in enumerate(pairs)]
    for copy in copies:
        copy.start()
    for copy in copies:
        copy.wait()
    below, above = [near_loop(place_ref[1], d, panel_ref.shape[0]) for d in (-1, 1)]
    total[0:cols, 0:BLK] += dot(panel_ref[below, CAP], edge_ref[0], NT)
    total[0:cols, rows - BLK :] += dot(panel_ref[above, CAP], edge_ref[1], NT)
    ones = jnp.ones((ONES, BLK), BF)
    for start in range(0, count, 8):
        terms = []
        for r in range(start, start + 8):
            key = key_ref[0, r]
            left = jnp.concatenate([panel_ref[key // CAP, key % CAP], ones], axis=0)
            terms.append(dot(left, a_ref[r], NT))
        for r in range(start, start + 8):
            where = lanes(row_ref[r])
            total[:, where] = total[:, where] + terms[r - start]
    part = m0.shape[1]
    for k, mean_ref in enumerate((m1, m2, m3, m0)):
        at = near_rows(feat, (k + 1) % 4, part)
        inverse = 1.0 / (1.0 + total[cols : cols + 1, at])
        mean_ref[...] = (total[0:cols, at] * inverse).astype(BF)
        if k == 3:
            inverse_ref[...] = inverse


def off_forward(place, row, key, band_sum, band, panels, off):
    cols, rows = panels.shape[2], band_sum.shape[1]
    mean = ((cols, rows // 4), BF)
    return call(
        off_kernel,
        "off_forward",
        "ssshhhv>vvvvv",
        (place, row, key, band_sum, band, panels, off),
        4 * (mean,) + (((1, rows // 4), F32),),
        scratch=[
            pltpu.VMEM(band_sum.shape, F32),
            pltpu.VMEM((2, BLK, BLK), BF),
            pltpu.VMEM(panels.shape, BF),
            DMA((4,)),
        ],
        flops=2 * off.shape[0] * BLK * BLK * (cols + ONES),
    )


def weights_kernel(place_ref, p0, p1, p2, p3, down_ref, bias_ref, back_ref):
    feat = place_ref[0]
    hidden = down_ref.shape[0]
    cols, part = back_ref.shape[0] // 8, hidden // 4
    here = lax.broadcasted_iota(I32, (hidden, hidden), 0)
    there = lax.broadcasted_iota(I32, (hidden, hidden), 1)
    place = (jnp.bitwise_xor(there // part, feat)) * part + there % part
    chosen = jnp.where(here == place, 0.5, 0.0).astype(BF)
    eye = lax.broadcasted_iota(I32, (part, part), 0) == lax.broadcasted_iota(
        I32, (part, part), 1
    )
    own, neigh = [], []
    for k, p in enumerate((p0, p1, p2, p3)):
        rows = slice(cols + part, cols + part + 16)
        for g in range(cols // 16):
            own.append(p[rows, 2 * g * hidden : (2 * g + 1) * hidden])
            neigh.append(p[rows, (2 * g + 1) * hidden : (2 * g + 2) * hidden])
        start = cols // 8 * hidden
        lines = p[rows, start : start + BLK].astype(F32)[:, 0:part]
        line = (lines[0:1] + lines[1:2]) + lines[2:3]
        bias_ref[k * part : (k + 1) * part, :] = 0.5 * jnp.sum(
            jnp.where(eye, line, 0.0), axis=1, keepdims=True
        )
    down_ref[...] = dot(chosen, jnp.concatenate(own + neigh, axis=0), TT).astype(BF)
    back_ref[...] = dot(jnp.concatenate(neigh + own, axis=0), chosen).astype(BF)


def weights(place, pieces, cols, hidden):
    return call(
        weights_kernel,
        "weights",
        "svvvv>vvv",
        (place, *pieces),
        (((hidden, 8 * cols), BF), ((hidden, 1), F32), ((8 * cols, hidden), BF)),
    )


def dense_kernel(
    p0, p1, p2, p3, m0, m1, m2, m3, inverse_ref, down_ref, bias_ref, back_w_ref,
    b0, b1, b2, b3, grad_ref, h0, h1, h2, h3, s0, s1, s2, s3, helds, selfs, sems,
):
    cols, rows = m0.shape
    pieces = (p0, p1, p2, p3)
    part = h0.shape[0]
    width = 2 * BLK

    def project(i):
        at = slice(i * width, (i + 1) * width)
        both = [p[0:cols, at] for p in pieces] + [m[:, at] for m in (m0, m1, m2, m3)]
        return dot(down_ref[...], jnp.concatenate(both, axis=0))

    def gradient(i, half):
        at = slice(i * width, (i + 1) * width)
        grads = []
        for k, p in enumerate(pieces):
            here = slice(k * part, (k + 1) * part)
            u = half[here] + bias_ref[here]
            t = jnp.tanh(u)
            s = 1.0 + t
            helds[k, :, at] = (u * s).astype(BF)
            c = p[cols : cols + part, at].astype(F32)
            grads.append((c * s * (1.0 + u * (1.0 - t))).astype(BF))
        return jnp.concatenate(grads, axis=0)

    def products(i, grad):
        at = slice(i * width, (i + 1) * width)
        grad_ref[:, at] = grad
        both = dot(back_w_ref[...], grad)
        backs = both[0 : 4 * cols] * inverse_ref[:, at]
        for k, b in enumerate((b0, b1, b2, b3)):
            b[:, at] = backs[k * cols : (k + 1) * cols].astype(BF)
            own = both[(4 + k) * cols : (5 + k) * cols]
            selfs[k, :, at] = own.astype(BF)

    count = rows // width
    half, grad = project(0), None
    for i in range(count):
        later = project(i + 1) if i + 1 < count else None
        fresh = gradient(i, half)
        if grad is not None:
            products(i - 1, grad)
        half, grad = later, fresh
    sends = []
    for k, h in enumerate((h0, h1, h2, h3)):
        sends.append(pltpu.make_async_copy(helds.at[k], h, sems.at[k]))
        sends[-1].start()
    products(count - 1, grad)
    for k, s in enumerate((s0, s1, s2, s3)):
        sends.append(pltpu.make_async_copy(selfs.at[k], s, sems.at[4 + k]))
        sends[-1].start()
    for send in sends:
        send.wait()


def dense(pieces, ms, inverse, down, bias, back_w):
    cols, rows = ms[0].shape
    hidden = down.shape[0]
    return call(
        dense_kernel,
        "dense",
        12 * "v" + ">vvvvvhhhhhhhh",
        (*pieces, *ms, inverse, down, bias, back_w),
        4 * (((cols, rows), BF),)
        + (((hidden, rows), BF),)
        + 4 * (((hidden // 4, rows), BF),)
        + 4 * (((cols, rows), BF),),
        scratch=[
            pltpu.VMEM((4, hidden // 4, rows), BF),
            pltpu.VMEM((4, cols, rows), BF),
            DMA((8,)),
        ],
        flops=2 * rows * hidden * 400,
    )


def after_kernel(feat_ref, p0, p1, p2, p3, m0, m1, m2, m3, grad_ref, g0, g1, g2, g3):
    cols, rows = m0.shape
    part = grad_ref.shape[0] // 4
    grad = grad_ref[...]
    left = [p[0:cols, :] for p in (p0, p1, p2, p3)] + [m[...] for m in (m0, m1, m2, m3)]
    left.append(jnp.ones((ONES, rows), BF))
    total = dot(jnp.concatenate(left, axis=0), grad, NT)
    feat = feat_ref[0]
    low, high = total[:, 0:BLK], total[:, BLK:]
    far = (feat & 2) != 0
    halves = [jnp.where(far, high, low), jnp.where(far, low, high)]
    halves = [jnp.where((feat & 1) != 0, pltpu.roll(h, part, 1), h) for h in halves]
    tall = 4 * cols
    for k, out in enumerate((g0, g1, g2, g3)):
        for h in range(2):
            at = slice(h * BLK, (h + 1) * BLK)
            out[0:cols, at] = halves[h][k * cols : (k + 1) * cols]
            out[cols : 2 * cols, at] = halves[h][tall + k * cols : tall + (k + 1) * cols]
        line = (low if k < 2 else high)[2 * tall : 2 * tall + 8]
        out[2 * cols :, 0:BLK] = pltpu.roll(line, part, 1) if k % 2 else line
        out[2 * cols :, BLK:] = jnp.zeros((8, BLK), F32)


def after(place, pieces, ms, grad):
    cols, _ = ms[0].shape
    return call(
        after_kernel,
        "after",
        "s" + 9 * "v" + ">wwww",
        (place, *pieces, *ms, grad),
        4 * (((2 * cols + 8, grad.shape[0]), F32),),
    )


def off_back_kernel(
    place_ref, row_ref, key_ref, b0, b1, b2, b3, a_ref, band_ref, out_ref, back_ref,
    held, edge_ref, sem, sems,
):
    count = band_ref.shape[0]
    edges = [
        pltpu.make_async_copy(band_ref.at[0, 0], edge_ref.at[0], sems.at[0]),
        pltpu.make_async_copy(band_ref.at[count - 1, 2], edge_ref.at[1], sems.at[1]),
    ]
    for edge in edges:
        edge.start()
    for k, b in enumerate((b0, b1, b2, b3)):
        back_ref[:, near_rows(place_ref[0], k, b.shape[1])] = b[...]
    held[...] = jnp.zeros_like(held)
    for r in range(a_ref.shape[0]):
        key = key_ref[0, r]
        left = back_ref[:, lanes(row_ref[r])]
        held[key // CAP, key % CAP] = dot(left, a_ref[r]).astype(BF)
    for edge in edges:
        edge.wait()
    below, above = [near_loop(place_ref[1], d, held.shape[0]) for d in (-1, 1)]
    rows = back_ref.shape[1]
    held[below, CAP] = dot(back_ref[:, 0:BLK], edge_ref[0]).astype(BF)
    held[above, CAP] = dot(back_ref[:, rows - BLK :], edge_ref[1]).astype(BF)
    copy = pltpu.make_async_copy(held, out_ref, sem)
    copy.start()
    copy.wait()


def off_backward(place, row, key, backs, off, band, loop_size):
    cols, part = backs[0].shape
    shape = (loop_size, SLOTS, cols, BLK)
    return call(
        off_back_kernel,
        "off_backward",
        "sssvvvvvh>hv",
        (place, row, key, *backs, off, band),
        ((shape, BF), ((cols, 4 * part), BF)),
        scratch=[pltpu.VMEM(shape, BF), pltpu.VMEM((2, BLK, BLK), BF), DMA, DMA((2,))],
    )


def band_back_kernel(back_ref, a_ref, total, held, sems):
    count, steps = a_ref.shape[0], sems.shape[0]
    group = count // steps
    copies = []
    for i in range(steps):
        at = pl.ds(i * group, group)
        copies.append(pltpu.make_async_copy(a_ref.at[at], held.at[at], sems.at[i]))
        copies[-1].start()
    carried = [None, None]
    for i in range(steps):
        copies[i].wait()
        for b in range(i * group, (i + 1) * group):
            right = jnp.concatenate([held[b, 0], held[b, 1], held[b, 2]], axis=1)
            term = dot(back_ref[:, b * BLK : (b + 1) * BLK], right)
            first, middle, last = [term[:, o * BLK : (o + 1) * BLK] for o in range(3)]
            if b > 0:
                total[:, (b - 1) * BLK : b * BLK] = carried[0] + first
            carried = [middle if b == 0 else carried[1] + middle, last]
    total[:, (count - 1) * BLK :] = carried[0]


def band_backward(back, band):
    cols, rows = back.shape
    (out,) = call(
        band_back_kernel,
        "band_backward",
        "vh>w",
        (back, band),
        (((cols, rows), F32),),
        scratch=[pltpu.VMEM(band.shape, BF), DMA((8,))],
    )
    return out


def collect_kernel(
    place_ref, asked_ref, start_ref, in_ref, h0, h1, h2, h3, s0, s1, s2, s3,
    out_ref, hidden_out, total, second, held, selfs, hidden_ref, table, sems, in_sems, out_sems,
):
    feat = place_ref[0]
    steps = in_sems.shape[0]
    group = held.shape[0] // steps

    def arrive(j):
        at = pl.ds(j * group, group)
        return pltpu.make_async_copy(in_ref.at[at], held.at[at], in_sems.at[j])

    rows, part = total.shape[1], h0.shape[1]
    copies = [
        pltpu.make_async_copy(asked_ref.at[:, 0, :], table, sems.at[0]),
        pltpu.make_async_copy(start_ref, total, sems.at[1]),
    ]
    for k, s in enumerate((s0, s1, s2, s3)):
        copies.append(pltpu.make_async_copy(s, selfs.at[k], sems.at[2 + k]))
    for k, h in enumerate((h0, h1, h2, h3)):
        at = near_rows(feat, k, part)
        copies.append(pltpu.make_async_copy(h, hidden_ref.at[:, at], sems.at[6 + k]))
    for copy in copies[:6]:
        copy.start()
    for j in range(steps):
        arrive(j).start()
    for copy in copies[6:]:
        copy.start()
    copies[1].wait()
    for k in range(4):
        copies[2 + k].wait()
        at = near_rows(feat, k, part)
        total[:, at] = total[:, at] + selfs[k].astype(F32)
    copies[0].wait()

    def body(p, carry):
        for s in range(CAP):
            at = lanes(table[p, s])
            sums = second if s % 2 else total
            sums[:, at] = sums[:, at] + held[p, s].astype(F32)
        return carry

    second[...] = jnp.zeros_like(second)
    sends = []
    for j in range(steps):
        arrive(j).wait()
        lax.fori_loop(j * group, (j + 1) * group, body, 0, unroll=4)
        copies[6 + j].wait()
        at = near_rows(feat, j, part)
        sends.append(
            pltpu.make_async_copy(hidden_ref.at[:, at], hidden_out.at[:, at], out_sems.at[j])
        )
        sends[-1].start()
    below, above = [near_loop(place_ref[1], d, held.shape[0]) for d in (-1, 1)]
    total[:, 0:BLK] += held[below, CAP].astype(F32)
    total[:, rows - BLK :] += held[above, CAP].astype(F32)
    out_ref[...] = (total[...] + second[...]).astype(BF)
    for send in sends:
        send.wait()


def collect(place, asked, band_sum, incoming, outs):
    cols, rows = band_sum.shape
    return call(
        collect_kernel,
        "collect",
        "saah" + 8 * "h" + ">wh",
        (place, asked, band_sum, incoming, *outs),
        ((band_sum.shape, BF), ((outs[0].shape[0], rows), BF)),
        scratch=[
            pltpu.VMEM(band_sum.shape, F32),
            pltpu.VMEM(band_sum.shape, F32),
            pltpu.VMEM(incoming.shape, BF),
            pltpu.VMEM((4, cols, rows // 4), BF),
            pltpu.VMEM((outs[0].shape[0], rows), BF),
            pltpu.SMEM((asked.shape[0], BLK), I32),
            DMA((10,)),
            DMA((4,)),
            DMA((4,)),
        ],
    )


def finish_kernel(scale, own_ref, other_ref, out_ref, bias_ref):
    total = (own_ref[...] + other_ref[...]) * scale
    tall = out_ref.shape[0]
    out_ref[...] = total[0:tall]
    bias_ref[...] = total[tall : tall + 1, 0 : bias_ref.shape[1]]


def finish(own, other, part, scale):
    tall, wide = own.shape
    return call(
        lambda *refs: finish_kernel(scale, *refs),
        "finish",
        "ww>ww",
        (own, other),
        (((tall - 8, wide), F32), ((1, part), F32)),
    )


def per_device(
    features, band_blocks, off_blocks, off_row, off_col, off_part, w_self, w_neigh, bias, cotangent
):
    rows, cols = features.shape
    loop_size = lax.axis_size("loop")
    together = lax.optimization_barrier

    def swap(value, k, j=0):
        pairs = [(4 * i + f, 4 * (i ^ j) + (f ^ k)) for i in range(loop_size) for f in range(4)]
        return lax.ppermute(value, ("loop", "feat"), pairs)

    def swapped(values):
        return [values[0]] + [swap(values[k], k) for k in (1, 2, 3)]

    def spread(value):
        return lax.all_to_all(value, "loop", split_axis=0, concat_axis=0, tiled=True)

    place = jnp.stack([lax.axis_index("feat"), lax.axis_index("loop")]).astype(I32)
    x, cot = features.T, cotangent.T
    key, request = prepare(off_part.reshape(1, -1), off_col.reshape(1, -1), loop_size)
    request, place = together((request, place))
    asked = spread(request)
    pieces = by_device(place, x, cot, w_self, w_neigh, bias.reshape(1, -1))
    asked, then = together((asked, pieces[0]))[0], place
    pieces = swapped(pieces)
    ready = answers(place, asked, x)
    ready, then = together((ready, then))
    panels = spread(ready)
    band_sum, off = band_forward(then, band_blocks, off_blocks, x)
    *ms, inverse = off_forward(place, off_row, key, band_sum, band_blocks, panels, off)
    ms = swapped(ms)
    down, bias_down, back_w = weights(place, pieces, cols, w_self.shape[1])
    ms, down = together((ms, down))
    *rest, h0, h1, h2, h3, s0, s1, s2, s3 = dense(pieces, ms, inverse, down, bias_down, back_w)
    *backs, grad = rest
    backs = swapped(backs)
    terms = after(place, pieces, ms, grad)
    near = swapped(terms)
    selfs = swapped([s0, s1, s2, s3])
    outgoing, back = off_backward(place, off_row, key, backs, off, band_blocks, loop_size)
    grads = (near[0] + near[1]) + (near[2] + near[3])
    one, two, three = [swap(grads, 0, j) for j in (8, 16, 24)]
    outs = [h0, h1, h2, h3]
    outgoing, back, one, two, three, selfs, outs = together(
        (outgoing, back, one, two, three, selfs, outs)
    )
    incoming = spread(outgoing)
    outs = [outs[0], outs[1], swap(outs[2], 2), swap(outs[3], 3)]
    back_sum = band_backward(back, band_blocks)
    grads = (grads + one) + (two + three)
    one, two, three = [swap(grads, 0, j) for j in (2, 4, 6)]
    one, two, three, outs[1] = together((one, two, three, outs[1]))
    outs[1] = swap(outs[1], 1)
    grads = (grads + one) + (two + three)
    other = swap(grads, 0, 1)
    grad_features, hidden = collect(place, asked, back_sum, incoming, outs + selfs)
    other, grad_features = together((other, grad_features))
    weight_grads, bias_grad = finish(
        grads, other, bias.shape[0], 0.5 / math.sqrt(rows * loop_size)
    )
    return (
        hidden.T,
        grad_features.T,
        weight_grads.reshape(2, cols, w_self.shape[1]),
        bias_grad.reshape(-1),
    )


def solution(mesh):
    return jax.shard_map(
        per_device,
        mesh=mesh,
        in_specs=(
            P("loop", "feat"),
            P("loop", None, None, None),
            P("loop", None, None),
            P("loop"),
            P("loop"),
            P("loop", None),
            P("feat", None),
            P("feat", None),
            P("feat"),
            P("loop", "feat"),
        ),
        out_specs=(P("loop", "feat"), P("loop", "feat"), P(None, "feat", None), P("feat")),
        check_vma=False,
    )
```

```python
import math

import jax
import jax.numpy as jnp
from jax import lax
from jax.experimental import pallas as pl
from jax.experimental.pallas import tpu as pltpu
from jax.sharding import PartitionSpec as P

BF = jnp.bfloat16
F32 = jnp.float32
I32 = jnp.int32
BLK = 128
ONES = 16
CAP = 4
SLOTS = CAP + 1
NN = (((1,), (0,)), ((), ()))
NT = (((1,), (1,)), ((), ()))
TT = (((0,), (1,)), ((), ()))
DMA = pltpu.SemaphoreType.DMA


def lanes(block, width=BLK):
    return pl.ds(pl.multiple_of(block * BLK, BLK), width)


def dot(a, b, dims=NN):
    return lax.dot_general(a, b, dims, preferred_element_type=F32)


def call(kernel, name, places, operands, results, scratch=(), aliases=None, flops=0, mib=16):
    spaces = {"v": pltpu.VMEM, "h": pltpu.HBM, "s": pltpu.SMEM, "a": pl.ANY, "w": pltpu.VMEM}
    ins, outs = places.split(">")
    held = [
        pltpu.with_memory_space_constraint(x, spaces[p]) if p in "vh" else x
        for p, x in zip(ins, operands, strict=True)
    ]
    nbytes = sum(math.prod(x.shape) * x.dtype.itemsize for x in operands)
    kinds = [
        {"v": pltpu.VMEM, "h": pltpu.HBM}.get(p, jax.ShapeDtypeStruct)(shape, dtype)
        for p, (shape, dtype) in zip(outs, results, strict=True)
    ]
    return pl.pallas_call(
        kernel,
        in_specs=[pl.BlockSpec(memory_space=spaces[p]) for p in ins],
        out_specs=[pl.BlockSpec(memory_space=spaces[p]) for p in outs],
        out_shape=kinds,
        scratch_shapes=list(scratch),
        input_output_aliases=aliases or {},
        compiler_params=pltpu.CompilerParams(vmem_limit_bytes=mib << 20),
        cost_estimate=pl.CostEstimate(flops=1, bytes_accessed=1, transcendentals=0),
        name=name,
    )(*held)


def near_rows(feat, k, rows):
    return pl.ds(pl.multiple_of(jnp.bitwise_xor(feat, k) * rows, BLK), rows)


def near_loop(me, shift, count):
    return lax.rem(me + shift + count, count)


def prepare_kernel(part_in, col_in, key_ref, request_ref, part_ref, col_ref, sems):
    copies = [
        pltpu.make_async_copy(part_in, part_ref, sems.at[0]),
        pltpu.make_async_copy(col_in, col_ref, sems.at[1]),
    ]
    for copy in copies:
        copy.start()
    for copy in copies:
        copy.wait()
    part, col = part_ref[...], col_ref[...]
    count = part.shape[1]
    first = lax.broadcasted_iota(I32, (count, count), 0)
    second = lax.broadcasted_iota(I32, (count, count), 1)
    part_down = jnp.sum(jnp.where(first == second, part, 0), axis=1, keepdims=True)
    earlier = (part_down == part) & (first < second)
    slot = jnp.sum(earlier.astype(I32), axis=0, keepdims=True)
    key_ref[...] = part * CAP + slot
    shape = request_ref.shape
    wide = (shape[0], shape[1], count)
    owner = lax.broadcasted_iota(I32, wide, 0)
    lane = lax.broadcasted_iota(I32, shape, 2)
    hit = owner == part[None]
    table = jnp.zeros(shape, I32)
    for s in range(CAP):
        value = jnp.sum(
            jnp.where(hit & (slot[None] == s), col[None], 0), axis=2, keepdims=True
        )
        table = jnp.where(lane == s, value, table)
    request_ref[...] = table


def prepare(part, col, loop_size):
    return call(
        prepare_kernel,
        "prepare",
        "hh>ww",
        (part, col),
        ((part.shape, I32), ((loop_size, 1, BLK), I32)),
        scratch=[pltpu.VMEM(part.shape, I32), pltpu.VMEM(col.shape, I32), DMA((2,))],
    )


def band_kernel(
    tie_ref, a_ref, off_ref, x_in, out_ref, off_held,
    band_ref, wide, total, sems, out_sems, more, x_sem,
):
    del tie_ref
    cols, rows = x_in.shape
    steps = sems.shape[0]
    group = a_ref.shape[0] // steps

    def copy(i):
        at = pl.ds(i * group, group)
        return pltpu.make_async_copy(a_ref.at[at], band_ref.at[at], sems.at[i])

    def send(i):
        at = lanes(i * group, group * BLK)
        return pltpu.make_async_copy(total.at[:, at], out_ref.at[:, at], out_sems.at[i])

    x_copy = pltpu.make_async_copy(x_in, wide.at[0:cols, BLK : BLK + rows], x_sem)
    x_copy.start()
    for i in range(steps):
        copy(i).start()
    late = pltpu.make_async_copy(off_ref, off_held, more)
    late.start()
    wide[0:cols, 0:BLK] = jnp.zeros((cols, BLK), BF)
    wide[0:cols, BLK + rows :] = jnp.zeros((cols, BLK), BF)
    wide[cols:, :] = jnp.ones((ONES, wide.shape[1]), BF)
    x_copy.wait()

    def body(i, carry):
        copy(i).wait()
        for r in range(group):
            b = i * group + r
            left = wide[:, lanes(b, 3 * BLK)]
            right = jnp.concatenate([band_ref[b, 0], band_ref[b, 1], band_ref[b, 2]], axis=1)
            total[:, lanes(b)] = dot(left, right, NT)
        send(i).start()
        return carry

    lax.fori_loop(0, steps, body, 0)
    for i in range(steps):
        send(i).wait()
    late.wait()


def band_forward(tie, band, off, x):
    cols, rows = x.shape
    return call(
        band_kernel,
        "band_forward",
        "shhh>hv",
        (tie, band, off, x),
        (((cols + ONES, rows), F32), (off.shape, BF)),
        scratch=[
            pltpu.VMEM(band.shape, BF),
            pltpu.VMEM((cols + ONES, rows + 2 * BLK), BF),
            pltpu.VMEM((cols + ONES, rows), F32),
            DMA((8,)),
            DMA((8,)),
            DMA,
            DMA,
        ],
        flops=2 * (cols + ONES) * 3 * BLK * rows,
    )


def pieces_kernel(
    place_ref, x_ref, cot_ref, self_in, neigh_in, bias_in, p0, p1, p2, p3,
    held, self_ref, neigh_ref, bias_ref, sems, out_sems, more,
):
    cols, part = x_ref.shape[0], cot_ref.shape[0]
    tall, rows = cols + part, x_ref.shape[1] // 4
    copies, sends = [], []
    for k, piece in enumerate((p0, p1, p2, p3)):
        at = near_rows(place_ref[0], k, rows)
        copies.append(
            pltpu.make_async_copy(x_ref.at[:, at], held.at[k, 0:cols, 0:rows], sems.at[2 * k])
        )
        copies.append(
            pltpu.make_async_copy(
                cot_ref.at[:, at], held.at[k, cols:tall, 0:rows], sems.at[2 * k + 1]
            )
        )
        sends.append(pltpu.make_async_copy(held.at[k], piece, out_sems.at[k]))
    small = [
        pltpu.make_async_copy(a, b, more.at[i])
        for i, (a, b) in enumerate(
            ((self_in, self_ref), (neigh_in, neigh_ref), (bias_in, bias_ref))
        )
    ]
    for copy in small:
        copy.start()
    for k in (1, 2, 3, 0):
        copies[2 * k].start()
        copies[2 * k + 1].start()
    for copy in small:
        copy.wait()
    hidden = self_ref.shape[1]
    bias = bias_ref[...]
    high = bias.astype(BF)
    rest = bias - high.astype(F32)
    middle = rest.astype(BF)
    low = (rest - middle.astype(F32)).astype(BF)
    row = lax.broadcasted_iota(I32, (16, part), 0)
    lines = [jnp.broadcast_to(v.astype(F32), (16, part)) for v in (high, middle, low)]
    lines = jnp.where(row == 0, lines[0], jnp.where(row == 1, lines[1], lines[2]))
    lines = jnp.where(row < 3, lines, 0.0).astype(BF)
    for k in range(4):
        held[k, 0:cols, rows:] = self_ref[...]
        held[k, cols : 2 * cols, rows:] = neigh_ref[...]
        held[k, 2 * cols :, rows:] = jnp.zeros((tall - 2 * cols, hidden), BF)
        held[k, 2 * cols : 2 * cols + 16, rows : rows + part] = lines
    for k in (1, 2, 3, 0):
        copies[2 * k].wait()
        copies[2 * k + 1].wait()
        sends[k].start()
    for send in sends:
        send.wait()


def by_device(place, x, cot, w_self, w_neigh, bias):
    piece = (x.shape[0] + cot.shape[0], x.shape[1] // 4 + w_self.shape[1])
    return call(
        pieces_kernel,
        "by_device",
        "shhhhh>hhhh",
        (place, x, cot, w_self, w_neigh, bias),
        4 * ((piece, BF),),
        scratch=[
            pltpu.VMEM((4, *piece), BF),
            pltpu.VMEM(w_self.shape, BF),
            pltpu.VMEM(w_neigh.shape, BF),
            pltpu.VMEM(bias.shape, F32),
            DMA((8,)),
            DMA((4,)),
            DMA((3,)),
        ],
    )


def answer_kernel(place_ref, asked_ref, x_in, out_ref, x_ref, held, table, sem, x_sem, sems):
    copy = pltpu.make_async_copy(asked_ref.at[:, 0, :], table, sem)
    x_copy = pltpu.make_async_copy(x_in, x_ref, x_sem)
    copy.start()
    x_copy.start()
    count, steps = held.shape[0], sems.shape[0]
    group = count // steps
    above = near_loop(place_ref[1], 1, count)

    def send(j):
        at = pl.ds(j * group, group)
        return pltpu.make_async_copy(held.at[at], out_ref.at[at], sems.at[j])

    def body(p, carry):
        for s in range(CAP):
            held[p, s] = x_ref[:, lanes(table[p, s])]
        edge = jnp.where(p == above, x_ref.shape[1] // BLK - 1, 0)
        held[p, CAP] = x_ref[:, lanes(edge)]
        return carry

    copy.wait()
    x_copy.wait()
    for j in range(steps):
        lax.fori_loop(j * group, (j + 1) * group, body, 0, unroll=4)
        send(j).start()
    for j in range(steps):
        send(j).wait()


def answers(place, asked, x):
    shape = (asked.shape[0], SLOTS, x.shape[0], BLK)
    (out,) = call(
        answer_kernel,
        "answers",
        "sah>h",
        (place, asked, x),
        ((shape, BF),),
        scratch=[
            pltpu.VMEM(x.shape, BF),
            pltpu.VMEM(shape, BF),
            pltpu.SMEM((shape[0], BLK), I32),
            DMA,
            DMA,
            DMA((4,)),
        ],
    )
    return out


def off_kernel(
    place_ref, row_ref, key_ref, start_in, band_in, panel_in, a_ref,
    m0, m1, m2, m3, inverse_ref, total, edge_ref, panel_ref, sems,
):
    feat = place_ref[0]
    cols, rows = m0.shape[0], total.shape[1]
    count = a_ref.shape[0]
    pairs = [
        (panel_in, panel_ref), (start_in, total),
        (band_in.at[0, 0], edge_ref.at[0]), (band_in.at[band_in.shape[0] - 1, 2], edge_ref.at[1]),
    ]
    copies = [pltpu.make_async_copy(a, b, sems.at[i]) for i, (a, b) in enumerate(pairs)]
    for copy in copies:
        copy.start()
    for copy in copies:
        copy.wait()
    below, above = [near_loop(place_ref[1], d, panel_ref.shape[0]) for d in (-1, 1)]
    total[0:cols, 0:BLK] += dot(panel_ref[below, CAP], edge_ref[0], NT)
    total[0:cols, rows - BLK :] += dot(panel_ref[above, CAP], edge_ref[1], NT)
    ones = jnp.ones((ONES, BLK), BF)
    for start in range(0, count, 8):
        terms = []
        for r in range(start, start + 8):
            key = key_ref[0, r]
            left = jnp.concatenate([panel_ref[key // CAP, key % CAP], ones], axis=0)
            terms.append(dot(left, a_ref[r], NT))
        for r in range(start, start + 8):
            where = lanes(row_ref[r])
            total[:, where] = total[:, where] + terms[r - start]
    part = m0.shape[1]
    for k, mean_ref in enumerate((m1, m2, m3, m0)):
        at = near_rows(feat, (k + 1) % 4, part)
        inverse = 1.0 / (1.0 + total[cols : cols + 1, at])
        mean_ref[...] = (total[0:cols, at] * inverse).astype(BF)
        if k == 3:
            inverse_ref[...] = inverse


def off_forward(place, row, key, band_sum, band, panels, off):
    cols, rows = panels.shape[2], band_sum.shape[1]
    mean = ((cols, rows // 4), BF)
    return call(
        off_kernel,
        "off_forward",
        "ssshhhv>vvvvv",
        (place, row, key, band_sum, band, panels, off),
        4 * (mean,) + (((1, rows // 4), F32),),
        scratch=[
            pltpu.VMEM(band_sum.shape, F32),
            pltpu.VMEM((2, BLK, BLK), BF),
            pltpu.VMEM(panels.shape, BF),
            DMA((4,)),
        ],
        flops=2 * off.shape[0] * BLK * BLK * (cols + ONES),
    )


def weights_kernel(place_ref, p0, p1, p2, p3, down_ref, bias_ref, back_ref):
    feat = place_ref[0]
    hidden = down_ref.shape[0]
    cols, part = back_ref.shape[0] // 8, hidden // 4
    here = lax.broadcasted_iota(I32, (hidden, hidden), 0)
    there = lax.broadcasted_iota(I32, (hidden, hidden), 1)
    place = (jnp.bitwise_xor(there // part, feat)) * part + there % part
    chosen = jnp.where(here == place, 0.5, 0.0).astype(BF)
    eye = lax.broadcasted_iota(I32, (part, part), 0) == lax.broadcasted_iota(
        I32, (part, part), 1
    )
    own, neigh = [], []
    for k, p in enumerate((p0, p1, p2, p3)):
        start = p.shape[1] - hidden
        own.append(p[0:cols, start:])
        neigh.append(p[cols : 2 * cols, start:])
        lines = p[2 * cols : 2 * cols + 16, start : start + BLK].astype(F32)[:, 0:part]
        line = (lines[0:1] + lines[1:2]) + lines[2:3]
        bias_ref[k * part : (k + 1) * part, :] = 0.5 * jnp.sum(
            jnp.where(eye, line, 0.0), axis=1, keepdims=True
        )
    down_ref[...] = dot(chosen, jnp.concatenate(own + neigh, axis=0), TT).astype(BF)
    back_ref[...] = dot(jnp.concatenate(neigh + own, axis=0), chosen).astype(BF)


def weights(place, pieces, cols, hidden):
    return call(
        weights_kernel,
        "weights",
        "svvvv>vvv",
        (place, *pieces),
        (((hidden, 8 * cols), BF), ((hidden, 1), F32), ((8 * cols, hidden), BF)),
    )


def dense_kernel(
    p0, p1, p2, p3, m0, m1, m2, m3, inverse_ref, down_ref, bias_ref, back_w_ref,
    b0, b1, b2, b3, grad_ref, h0, h1, h2, h3, s0, s1, s2, s3, helds, selfs, sems,
):
    cols, rows = m0.shape
    pieces = (p0, p1, p2, p3)
    part = h0.shape[0]
    width = 2 * BLK

    def project(i):
        at = slice(i * width, (i + 1) * width)
        both = [p[0:cols, at] for p in pieces] + [m[:, at] for m in (m0, m1, m2, m3)]
        return dot(down_ref[...], jnp.concatenate(both, axis=0))

    def gradient(i, half):
        at = slice(i * width, (i + 1) * width)
        grads = []
        for k, p in enumerate(pieces):
            here = slice(k * part, (k + 1) * part)
            u = half[here] + bias_ref[here]
            t = jnp.tanh(u)
            s = 1.0 + t
            helds[k, :, at] = (u * s).astype(BF)
            c = p[cols : cols + part, at].astype(F32)
            grads.append((c * s * (1.0 + u * (1.0 - t))).astype(BF))
        return jnp.concatenate(grads, axis=0)

    def products(i, grad):
        at = slice(i * width, (i + 1) * width)
        grad_ref[:, at] = grad
        both = dot(back_w_ref[...], grad)
        backs = both[0 : 4 * cols] * inverse_ref[:, at]
        for k, b in enumerate((b0, b1, b2, b3)):
            b[:, at] = backs[k * cols : (k + 1) * cols].astype(BF)
            own = both[(4 + k) * cols : (5 + k) * cols]
            selfs[k, :, at] = own.astype(BF)

    count = rows // width
    half, grad = project(0), None
    for i in range(count):
        later = project(i + 1) if i + 1 < count else None
        fresh = gradient(i, half)
        if grad is not None:
            products(i - 1, grad)
        half, grad = later, fresh
    sends = []
    for k, h in enumerate((h0, h1, h2, h3)):
        sends.append(pltpu.make_async_copy(helds.at[k], h, sems.at[k]))
        sends[-1].start()
    products(count - 1, grad)
    for k, s in enumerate((s0, s1, s2, s3)):
        sends.append(pltpu.make_async_copy(selfs.at[k], s, sems.at[4 + k]))
        sends[-1].start()
    for send in sends:
        send.wait()


def dense(pieces, ms, inverse, down, bias, back_w):
    cols, rows = ms[0].shape
    hidden = down.shape[0]
    return call(
        dense_kernel,
        "dense",
        12 * "v" + ">vvvvvhhhhhhhh",
        (*pieces, *ms, inverse, down, bias, back_w),
        4 * (((cols, rows), BF),)
        + (((hidden, rows), BF),)
        + 4 * (((hidden // 4, rows), BF),)
        + 4 * (((cols, rows), BF),),
        scratch=[
            pltpu.VMEM((4, hidden // 4, rows), BF),
            pltpu.VMEM((4, cols, rows), BF),
            DMA((8,)),
        ],
        flops=2 * rows * hidden * 400,
    )


def after_kernel(feat_ref, p0, p1, p2, p3, m0, m1, m2, m3, grad_ref, g0, g1, g2, g3):
    cols, rows = m0.shape
    part = grad_ref.shape[0] // 4
    grad = grad_ref[...]
    left = [p[0:cols, 0:rows] for p in (p0, p1, p2, p3)] + [m[...] for m in (m0, m1, m2, m3)]
    left.append(jnp.ones((ONES, rows), BF))
    total = dot(jnp.concatenate(left, axis=0), grad, NT)
    feat = feat_ref[0]
    low, high = total[:, 0:BLK], total[:, BLK:]
    far = (feat & 2) != 0
    halves = [jnp.where(far, high, low), jnp.where(far, low, high)]
    halves = [jnp.where((feat & 1) != 0, pltpu.roll(h, part, 1), h) for h in halves]
    tall = 4 * cols
    for k, out in enumerate((g0, g1, g2, g3)):
        for h in range(2):
            at = slice(h * BLK, (h + 1) * BLK)
            out[0:cols, at] = halves[h][k * cols : (k + 1) * cols]
            out[cols : 2 * cols, at] = halves[h][tall + k * cols : tall + (k + 1) * cols]
        line = (low if k < 2 else high)[2 * tall : 2 * tall + 8]
        out[2 * cols :, 0:BLK] = pltpu.roll(line, part, 1) if k % 2 else line
        out[2 * cols :, BLK:] = jnp.zeros((8, BLK), F32)


def after(place, pieces, ms, grad):
    cols, _ = ms[0].shape
    return call(
        after_kernel,
        "after",
        "s" + 9 * "v" + ">wwww",
        (place, *pieces, *ms, grad),
        4 * (((2 * cols + 8, grad.shape[0]), F32),),
    )


def off_back_kernel(
    place_ref, row_ref, key_ref, b0, b1, b2, b3, a_ref, band_ref, out_ref, back_ref,
    held, edge_ref, sem, sems,
):
    count = band_ref.shape[0]
    edges = [
        pltpu.make_async_copy(band_ref.at[0, 0], edge_ref.at[0], sems.at[0]),
        pltpu.make_async_copy(band_ref.at[count - 1, 2], edge_ref.at[1], sems.at[1]),
    ]
    for edge in edges:
        edge.start()
    for k, b in enumerate((b0, b1, b2, b3)):
        back_ref[:, near_rows(place_ref[0], k, b.shape[1])] = b[...]
    held[...] = jnp.zeros_like(held)
    for r in range(a_ref.shape[0]):
        key = key_ref[0, r]
        left = back_ref[:, lanes(row_ref[r])]
        held[key // CAP, key % CAP] = dot(left, a_ref[r]).astype(BF)
    for edge in edges:
        edge.wait()
    below, above = [near_loop(place_ref[1], d, held.shape[0]) for d in (-1, 1)]
    rows = back_ref.shape[1]
    held[below, CAP] = dot(back_ref[:, 0:BLK], edge_ref[0]).astype(BF)
    held[above, CAP] = dot(back_ref[:, rows - BLK :], edge_ref[1]).astype(BF)
    copy = pltpu.make_async_copy(held, out_ref, sem)
    copy.start()
    copy.wait()


def off_backward(place, row, key, backs, off, band, loop_size):
    cols, part = backs[0].shape
    shape = (loop_size, SLOTS, cols, BLK)
    return call(
        off_back_kernel,
        "off_backward",
        "sssvvvvvh>hv",
        (place, row, key, *backs, off, band),
        ((shape, BF), ((cols, 4 * part), BF)),
        scratch=[pltpu.VMEM(shape, BF), pltpu.VMEM((2, BLK, BLK), BF), DMA, DMA((2,))],
    )


def band_back_kernel(back_ref, a_ref, total, held, sems):
    count, steps = a_ref.shape[0], sems.shape[0]
    group = count // steps
    copies = []
    for i in range(steps):
        at = pl.ds(i * group, group)
        copies.append(pltpu.make_async_copy(a_ref.at[at], held.at[at], sems.at[i]))
        copies[-1].start()
    carried = [None, None]
    for i in range(steps):
        copies[i].wait()
        for b in range(i * group, (i + 1) * group):
            right = jnp.concatenate([held[b, 0], held[b, 1], held[b, 2]], axis=1)
            term = dot(back_ref[:, b * BLK : (b + 1) * BLK], right)
            first, middle, last = [term[:, o * BLK : (o + 1) * BLK] for o in range(3)]
            if b > 0:
                total[:, (b - 1) * BLK : b * BLK] = carried[0] + first
            carried = [middle if b == 0 else carried[1] + middle, last]
    total[:, (count - 1) * BLK :] = carried[0]


def band_backward(back, band):
    cols, rows = back.shape
    (out,) = call(
        band_back_kernel,
        "band_backward",
        "vh>w",
        (back, band),
        (((cols, rows), F32),),
        scratch=[pltpu.VMEM(band.shape, BF), DMA((8,))],
    )
    return out


def collect_kernel(
    place_ref, asked_ref, start_ref, in_ref, h0, h1, h2, h3, s0, s1, s2, s3,
    out_ref, hidden_out, total, second, held, selfs, hidden_ref, table, sems, in_sems, out_sems,
):
    feat = place_ref[0]
    steps = in_sems.shape[0]
    group = held.shape[0] // steps

    def arrive(j):
        at = pl.ds(j * group, group)
        return pltpu.make_async_copy(in_ref.at[at], held.at[at], in_sems.at[j])

    rows, part = total.shape[1], h0.shape[1]
    copies = [
        pltpu.make_async_copy(asked_ref.at[:, 0, :], table, sems.at[0]),
        pltpu.make_async_copy(start_ref, total, sems.at[1]),
    ]
    for k, s in enumerate((s0, s1, s2, s3)):
        copies.append(pltpu.make_async_copy(s, selfs.at[k], sems.at[2 + k]))
    for k, h in enumerate((h0, h1, h2, h3)):
        at = near_rows(feat, k, part)
        copies.append(pltpu.make_async_copy(h, hidden_ref.at[:, at], sems.at[6 + k]))
    for copy in copies[:6]:
        copy.start()
    for j in range(steps):
        arrive(j).start()
    for copy in copies[6:]:
        copy.start()
    copies[1].wait()
    for k in range(4):
        copies[2 + k].wait()
        at = near_rows(feat, k, part)
        total[:, at] = total[:, at] + selfs[k].astype(F32)
    copies[0].wait()

    def body(p, carry):
        for s in range(CAP):
            at = lanes(table[p, s])
            sums = second if s % 2 else total
            sums[:, at] = sums[:, at] + held[p, s].astype(F32)
        return carry

    second[...] = jnp.zeros_like(second)
    sends = []
    for j in range(steps):
        arrive(j).wait()
        lax.fori_loop(j * group, (j + 1) * group, body, 0, unroll=4)
        copies[6 + j].wait()
        at = near_rows(feat, j, part)
        sends.append(
            pltpu.make_async_copy(hidden_ref.at[:, at], hidden_out.at[:, at], out_sems.at[j])
        )
        sends[-1].start()
    below, above = [near_loop(place_ref[1], d, held.shape[0]) for d in (-1, 1)]
    total[:, 0:BLK] += held[below, CAP].astype(F32)
    total[:, rows - BLK :] += held[above, CAP].astype(F32)
    out_ref[...] = (total[...] + second[...]).astype(BF)
    for send in sends:
        send.wait()


def collect(place, asked, band_sum, incoming, outs):
    cols, rows = band_sum.shape
    return call(
        collect_kernel,
        "collect",
        "saah" + 8 * "h" + ">wh",
        (place, asked, band_sum, incoming, *outs),
        ((band_sum.shape, BF), ((outs[0].shape[0], rows), BF)),
        scratch=[
            pltpu.VMEM(band_sum.shape, F32),
            pltpu.VMEM(band_sum.shape, F32),
            pltpu.VMEM(incoming.shape, BF),
            pltpu.VMEM((4, cols, rows // 4), BF),
            pltpu.VMEM((outs[0].shape[0], rows), BF),
            pltpu.SMEM((asked.shape[0], BLK), I32),
            DMA((10,)),
            DMA((4,)),
            DMA((4,)),
        ],
    )


def finish_kernel(scale, own_ref, other_ref, out_ref, bias_ref):
    total = (own_ref[...] + other_ref[...]) * scale
    tall = out_ref.shape[0]
    out_ref[...] = total[0:tall]
    bias_ref[...] = total[tall : tall + 1, 0 : bias_ref.shape[1]]


def finish(own, other, part, scale):
    tall, wide = own.shape
    return call(
        lambda *refs: finish_kernel(scale, *refs),
        "finish",
        "ww>ww",
        (own, other),
        (((tall - 8, wide), F32), ((1, part), F32)),
    )


def per_device(
    features, band_blocks, off_blocks, off_row, off_col, off_part, w_self, w_neigh, bias, cotangent
):
    rows, cols = features.shape
    loop_size = lax.axis_size("loop")
    together = lax.optimization_barrier

    def swap(value, k, j=0):
        pairs = [(4 * i + f, 4 * (i ^ j) + (f ^ k)) for i in range(loop_size) for f in range(4)]
        return lax.ppermute(value, ("loop", "feat"), pairs)

    def swapped(values):
        return [values[0]] + [swap(values[k], k) for k in (1, 2, 3)]

    def spread(value):
        return lax.all_to_all(value, "loop", split_axis=0, concat_axis=0, tiled=True)

    place = jnp.stack([lax.axis_index("feat"), lax.axis_index("loop")]).astype(I32)
    x, cot = features.T, cotangent.T
    key, request = prepare(off_part.reshape(1, -1), off_col.reshape(1, -1), loop_size)
    request, place = together((request, place))
    asked = spread(request)
    pieces = by_device(place, x, cot, w_self, w_neigh, bias.reshape(1, -1))
    asked, then = together((asked, pieces[0]))[0], place
    pieces = swapped(pieces)
    ready = answers(place, asked, x)
    ready, then = together((ready, then))
    panels = spread(ready)
    band_sum, off = band_forward(then, band_blocks, off_blocks, x)
    *ms, inverse = off_forward(place, off_row, key, band_sum, band_blocks, panels, off)
    ms = swapped(ms)
    down, bias_down, back_w = weights(place, pieces, cols, w_self.shape[1])
    ms, down = together((ms, down))
    *rest, h0, h1, h2, h3, s0, s1, s2, s3 = dense(pieces, ms, inverse, down, bias_down, back_w)
    *backs, grad = rest
    backs = swapped(backs)
    terms = after(place, pieces, ms, grad)
    near = swapped(terms)
    selfs = [s0, s1, swap(s2, 2), swap(s3, 3)]
    outgoing, back = off_backward(place, off_row, key, backs, off, band_blocks, loop_size)
    grads = (near[0] + near[1]) + (near[2] + near[3])
    one, two, three = [swap(grads, 0, j) for j in (8, 16, 24)]
    outs = [h0, h1, h2, h3]
    grads = (grads + one) + (two + three)
    outgoing, back, grads, selfs, outs = together((outgoing, back, grads, selfs, outs))
    incoming = spread(outgoing)
    outs = [outs[0], outs[1], swap(outs[2], 2), swap(outs[3], 3)]
    back_sum = band_backward(back, band_blocks)
    one, two, three = [swap(grads, 0, j) for j in (2, 4, 6)]
    one, two, three, outs[1], selfs[1] = together((one, two, three, outs[1], selfs[1]))
    outs[1], selfs[1] = swap(outs[1], 1), swap(selfs[1], 1)
    grads = (grads + one) + (two + three)
    other = swap(grads, 0, 1)
    grad_features, hidden = collect(place, asked, back_sum, incoming, outs + selfs)
    other, grad_features = together((other, grad_features))
    weight_grads, bias_grad = finish(
        grads, other, bias.shape[0], 0.5 / math.sqrt(rows * loop_size)
    )
    return (
        hidden.T,
        grad_features.T,
        weight_grads.reshape(2, cols, w_self.shape[1]),
        bias_grad.reshape(-1),
    )


def solution(mesh):
    return jax.shard_map(
        per_device,
        mesh=mesh,
        in_specs=(
            P("loop", "feat"),
            P("loop", None, None, None),
            P("loop", None, None),
            P("loop"),
            P("loop"),
            P("loop", None),
            P("feat", None),
            P("feat", None),
            P("feat"),
            P("loop", "feat"),
        ),
        out_specs=(P("loop", "feat"), P("loop", "feat"), P(None, "feat", None), P("feat")),
        check_vma=False,
    )
```

```python
import math

import jax
import jax.numpy as jnp
from jax import lax
from jax.experimental import pallas as pl
from jax.experimental.pallas import tpu as pltpu
from jax.sharding import PartitionSpec as P

BF = jnp.bfloat16
F32 = jnp.float32
I32 = jnp.int32
BLK = 128
ONES = 16
CAP = 4
SLOTS = CAP + 1
NN = (((1,), (0,)), ((), ()))
NT = (((1,), (1,)), ((), ()))
TT = (((0,), (1,)), ((), ()))
DMA = pltpu.SemaphoreType.DMA


def lanes(block, width=BLK):
    return pl.ds(pl.multiple_of(block * BLK, BLK), width)


def dot(a, b, dims=NN):
    return lax.dot_general(a, b, dims, preferred_element_type=F32)


def call(kernel, name, places, operands, results, scratch=(), aliases=None, flops=0, mib=16):
    spaces = {"v": pltpu.VMEM, "h": pltpu.HBM, "s": pltpu.SMEM, "a": pl.ANY, "w": pltpu.VMEM}
    ins, outs = places.split(">")
    held = [
        pltpu.with_memory_space_constraint(x, spaces[p]) if p in "vh" else x
        for p, x in zip(ins, operands, strict=True)
    ]
    nbytes = sum(math.prod(x.shape) * x.dtype.itemsize for x in operands)
    kinds = [
        {"v": pltpu.VMEM, "h": pltpu.HBM}.get(p, jax.ShapeDtypeStruct)(shape, dtype)
        for p, (shape, dtype) in zip(outs, results, strict=True)
    ]
    return pl.pallas_call(
        kernel,
        in_specs=[pl.BlockSpec(memory_space=spaces[p]) for p in ins],
        out_specs=[pl.BlockSpec(memory_space=spaces[p]) for p in outs],
        out_shape=kinds,
        scratch_shapes=list(scratch),
        input_output_aliases=aliases or {},
        compiler_params=pltpu.CompilerParams(vmem_limit_bytes=mib << 20),
        cost_estimate=pl.CostEstimate(flops=1, bytes_accessed=1, transcendentals=0),
        name=name,
    )(*held)


def near_rows(feat, k, rows):
    return pl.ds(pl.multiple_of(jnp.bitwise_xor(feat, k) * rows, BLK), rows)


def near_loop(me, shift, count):
    return lax.rem(me + shift + count, count)


def prepare_kernel(part_in, col_in, key_ref, request_ref, part_ref, col_ref, sems):
    copies = [
        pltpu.make_async_copy(part_in, part_ref, sems.at[0]),
        pltpu.make_async_copy(col_in, col_ref, sems.at[1]),
    ]
    for copy in copies:
        copy.start()
    for copy in copies:
        copy.wait()
    part, col = part_ref[...], col_ref[...]
    count = part.shape[1]
    first = lax.broadcasted_iota(I32, (count, count), 0)
    second = lax.broadcasted_iota(I32, (count, count), 1)
    part_down = jnp.sum(jnp.where(first == second, part, 0), axis=1, keepdims=True)
    earlier = (part_down == part) & (first < second)
    slot = jnp.sum(earlier.astype(I32), axis=0, keepdims=True)
    key_ref[...] = part * CAP + slot
    shape = request_ref.shape
    wide = (shape[0], shape[1], count)
    owner = lax.broadcasted_iota(I32, wide, 0)
    lane = lax.broadcasted_iota(I32, shape, 2)
    hit = owner == part[None]
    table = jnp.zeros(shape, I32)
    for s in range(CAP):
        value = jnp.sum(
            jnp.where(hit & (slot[None] == s), col[None], 0), axis=2, keepdims=True
        )
        table = jnp.where(lane == s, value, table)
    request_ref[...] = table


def prepare(part, col, loop_size):
    return call(
        prepare_kernel,
        "prepare",
        "hh>ww",
        (part, col),
        ((part.shape, I32), ((loop_size, 1, BLK), I32)),
        scratch=[pltpu.VMEM(part.shape, I32), pltpu.VMEM(col.shape, I32), DMA((2,))],
    )


def band_kernel(
    tie_ref, a_ref, off_ref, x_in, out_ref, off_held,
    band_ref, wide, total, sems, out_sems, more, x_sem,
):
    del tie_ref
    cols, rows = x_in.shape
    steps = sems.shape[0]
    group = a_ref.shape[0] // steps

    def copy(i):
        at = pl.ds(i * group, group)
        return pltpu.make_async_copy(a_ref.at[at], band_ref.at[at], sems.at[i])

    def send(i):
        at = lanes(i * group, group * BLK)
        return pltpu.make_async_copy(total.at[:, at], out_ref.at[:, at], out_sems.at[i])

    x_copy = pltpu.make_async_copy(x_in, wide.at[0:cols, BLK : BLK + rows], x_sem)
    x_copy.start()
    for i in range(steps):
        copy(i).start()
    late = pltpu.make_async_copy(off_ref, off_held, more)
    late.start()
    wide[0:cols, 0:BLK] = jnp.zeros((cols, BLK), BF)
    wide[0:cols, BLK + rows :] = jnp.zeros((cols, BLK), BF)
    wide[cols:, :] = jnp.ones((ONES, wide.shape[1]), BF)
    x_copy.wait()

    def body(i, carry):
        copy(i).wait()
        for r in range(group):
            b = i * group + r
            left = wide[:, lanes(b, 3 * BLK)]
            right = jnp.concatenate([band_ref[b, 0], band_ref[b, 1], band_ref[b, 2]], axis=1)
            total[:, lanes(b)] = dot(left, right, NT)
        send(i).start()
        return carry

    lax.fori_loop(0, steps, body, 0)
    for i in range(steps):
        send(i).wait()
    late.wait()


def band_forward(tie, band, off, x):
    cols, rows = x.shape
    return call(
        band_kernel,
        "band_forward",
        "shhh>hv",
        (tie, band, off, x),
        (((cols + ONES, rows), F32), (off.shape, BF)),
        scratch=[
            pltpu.VMEM(band.shape, BF),
            pltpu.VMEM((cols + ONES, rows + 2 * BLK), BF),
            pltpu.VMEM((cols + ONES, rows), F32),
            DMA((8,)),
            DMA((8,)),
            DMA,
            DMA,
        ],
        flops=2 * (cols + ONES) * 3 * BLK * rows,
    )


def pieces_kernel(
    place_ref, x_ref, cot_ref, self_in, neigh_in, bias_in, p0, p1, p2, p3,
    held, self_ref, neigh_ref, bias_ref, sems, out_sems, more,
):
    cols, part = x_ref.shape[0], cot_ref.shape[0]
    tall, rows = cols + part, x_ref.shape[1] // 4
    copies, sends = [], []
    for k, piece in enumerate((p0, p1, p2, p3)):
        at = near_rows(place_ref[0], k, rows)
        copies.append(
            pltpu.make_async_copy(x_ref.at[:, at], held.at[k, 0:cols, 0:rows], sems.at[2 * k])
        )
        copies.append(
            pltpu.make_async_copy(
                cot_ref.at[:, at], held.at[k, cols:tall, 0:rows], sems.at[2 * k + 1]
            )
        )
        sends.append(pltpu.make_async_copy(held.at[k], piece, out_sems.at[k]))
    small = [
        pltpu.make_async_copy(a, b, more.at[i])
        for i, (a, b) in enumerate(
            ((self_in, self_ref), (neigh_in, neigh_ref), (bias_in, bias_ref))
        )
    ]
    for copy in small:
        copy.start()
    for k in (1, 2, 3, 0):
        copies[2 * k].start()
        copies[2 * k + 1].start()
    for copy in small:
        copy.wait()
    hidden = self_ref.shape[1]
    bias = bias_ref[...]
    high = bias.astype(BF)
    rest = bias - high.astype(F32)
    middle = rest.astype(BF)
    low = (rest - middle.astype(F32)).astype(BF)
    row = lax.broadcasted_iota(I32, (16, part), 0)
    lines = [jnp.broadcast_to(v.astype(F32), (16, part)) for v in (high, middle, low)]
    lines = jnp.where(row == 0, lines[0], jnp.where(row == 1, lines[1], lines[2]))
    lines = jnp.where(row < 3, lines, 0.0).astype(BF)
    for k in range(4):
        held[k, 0:cols, rows:] = self_ref[...]
        held[k, cols : 2 * cols, rows:] = neigh_ref[...]
        held[k, 2 * cols :, rows:] = jnp.zeros((tall - 2 * cols, hidden), BF)
        held[k, 2 * cols : 2 * cols + 16, rows : rows + part] = lines
    for k in (1, 2, 3, 0):
        copies[2 * k].wait()
        copies[2 * k + 1].wait()
        sends[k].start()
    for send in sends:
        send.wait()


def by_device(place, x, cot, w_self, w_neigh, bias):
    piece = (x.shape[0] + cot.shape[0], x.shape[1] // 4 + w_self.shape[1])
    return call(
        pieces_kernel,
        "by_device",
        "shhhhh>hhhh",
        (place, x, cot, w_self, w_neigh, bias),
        4 * ((piece, BF),),
        scratch=[
            pltpu.VMEM((4, *piece), BF),
            pltpu.VMEM(w_self.shape, BF),
            pltpu.VMEM(w_neigh.shape, BF),
            pltpu.VMEM(bias.shape, F32),
            DMA((8,)),
            DMA((4,)),
            DMA((3,)),
        ],
    )


def answer_kernel(place_ref, asked_ref, x_in, out_ref, x_ref, held, table, sem, x_sem, sems):
    copy = pltpu.make_async_copy(asked_ref.at[:, 0, :], table, sem)
    x_copy = pltpu.make_async_copy(x_in, x_ref, x_sem)
    copy.start()
    x_copy.start()
    count, steps = held.shape[0], sems.shape[0]
    group = count // steps
    above = near_loop(place_ref[1], 1, count)

    def send(j):
        at = pl.ds(j * group, group)
        return pltpu.make_async_copy(held.at[at], out_ref.at[at], sems.at[j])

    def body(p, carry):
        for s in range(CAP):
            held[p, s] = x_ref[:, lanes(table[p, s])]
        edge = jnp.where(p == above, x_ref.shape[1] // BLK - 1, 0)
        held[p, CAP] = x_ref[:, lanes(edge)]
        return carry

    copy.wait()
    x_copy.wait()
    for j in range(steps):
        lax.fori_loop(j * group, (j + 1) * group, body, 0, unroll=4)
        send(j).start()
    for j in range(steps):
        send(j).wait()


def answers(place, asked, x):
    shape = (asked.shape[0], SLOTS, x.shape[0], BLK)
    (out,) = call(
        answer_kernel,
        "answers",
        "sah>h",
        (place, asked, x),
        ((shape, BF),),
        scratch=[
            pltpu.VMEM(x.shape, BF),
            pltpu.VMEM(shape, BF),
            pltpu.SMEM((shape[0], BLK), I32),
            DMA,
            DMA,
            DMA((4,)),
        ],
    )
    return out


def off_kernel(
    place_ref, row_ref, key_ref, start_in, band_in, panel_in, a_ref,
    m0, m1, m2, m3, inverse_ref, total, edge_ref, panel_ref, sems,
):
    feat = place_ref[0]
    cols, rows = m0.shape[0], total.shape[1]
    count = a_ref.shape[0]
    pairs = [
        (panel_in, panel_ref), (start_in, total),
        (band_in.at[0, 0], edge_ref.at[0]), (band_in.at[band_in.shape[0] - 1, 2], edge_ref.at[1]),
    ]
    copies = [pltpu.make_async_copy(a, b, sems.at[i]) for i, (a, b) in enumerate(pairs)]
    for copy in copies:
        copy.start()
    for copy in copies:
        copy.wait()
    below, above = [near_loop(place_ref[1], d, panel_ref.shape[0]) for d in (-1, 1)]
    total[0:cols, 0:BLK] += dot(panel_ref[below, CAP], edge_ref[0], NT)
    total[0:cols, rows - BLK :] += dot(panel_ref[above, CAP], edge_ref[1], NT)
    ones = jnp.ones((ONES, BLK), BF)
    for start in range(0, count, 8):
        terms = []
        for r in range(start, start + 8):
            key = key_ref[0, r]
            left = jnp.concatenate([panel_ref[key // CAP, key % CAP], ones], axis=0)
            terms.append(dot(left, a_ref[r], NT))
        for r in range(start, start + 8):
            where = lanes(row_ref[r])
            total[:, where] = total[:, where] + terms[r - start]
    part = m0.shape[1]
    for k, mean_ref in enumerate((m1, m2, m3, m0)):
        at = near_rows(feat, (k + 1) % 4, part)
        inverse = 1.0 / (1.0 + total[cols : cols + 1, at])
        mean_ref[...] = (total[0:cols, at] * inverse).astype(BF)
        if k == 3:
            inverse_ref[...] = inverse


def off_forward(place, row, key, band_sum, band, panels, off):
    cols, rows = panels.shape[2], band_sum.shape[1]
    mean = ((cols, rows // 4), BF)
    return call(
        off_kernel,
        "off_forward",
        "ssshhhv>vvvvv",
        (place, row, key, band_sum, band, panels, off),
        4 * (mean,) + (((1, rows // 4), F32),),
        scratch=[
            pltpu.VMEM(band_sum.shape, F32),
            pltpu.VMEM((2, BLK, BLK), BF),
            pltpu.VMEM(panels.shape, BF),
            DMA((4,)),
        ],
        flops=2 * off.shape[0] * BLK * BLK * (cols + ONES),
    )


def weights_kernel(place_ref, p0, p1, p2, p3, down_ref, bias_ref, back_ref):
    feat = place_ref[0]
    hidden = down_ref.shape[0]
    cols, part = back_ref.shape[0] // 8, hidden // 4
    here = lax.broadcasted_iota(I32, (hidden, hidden), 0)
    there = lax.broadcasted_iota(I32, (hidden, hidden), 1)
    place = (jnp.bitwise_xor(there // part, feat)) * part + there % part
    chosen = jnp.where(here == place, 0.5, 0.0).astype(BF)
    eye = lax.broadcasted_iota(I32, (part, part), 0) == lax.broadcasted_iota(
        I32, (part, part), 1
    )
    own, neigh = [], []
    for k, p in enumerate((p0, p1, p2, p3)):
        start = p.shape[1] - hidden
        own.append(p[0:cols, start:])
        neigh.append(p[cols : 2 * cols, start:])
        lines = p[2 * cols : 2 * cols + 16, start : start + BLK].astype(F32)[:, 0:part]
        line = (lines[0:1] + lines[1:2]) + lines[2:3]
        bias_ref[k * part : (k + 1) * part, :] = 0.5 * jnp.sum(
            jnp.where(eye, line, 0.0), axis=1, keepdims=True
        )
    down_ref[...] = dot(chosen, jnp.concatenate(own + neigh, axis=0), TT).astype(BF)
    back_ref[...] = dot(jnp.concatenate(neigh + own, axis=0), chosen).astype(BF)


def weights(place, pieces, cols, hidden):
    return call(
        weights_kernel,
        "weights",
        "svvvv>vvv",
        (place, *pieces),
        (((hidden, 8 * cols), BF), ((hidden, 1), F32), ((8 * cols, hidden), BF)),
    )


def dense_kernel(
    p0, p1, p2, p3, m0, m1, m2, m3, inverse_ref, down_ref, bias_ref, back_w_ref,
    b0, b1, b2, b3, grad_ref, h0, h1, h2, h3, s0, s1, s2, s3, helds, selfs, sems,
):
    cols, rows = m0.shape
    pieces = (p0, p1, p2, p3)
    part = h0.shape[0]
    width = 2 * BLK

    def project(i):
        at = slice(i * width, (i + 1) * width)
        both = [p[0:cols, at] for p in pieces] + [m[:, at] for m in (m0, m1, m2, m3)]
        return dot(down_ref[...], jnp.concatenate(both, axis=0))

    def gradient(i, half):
        at = slice(i * width, (i + 1) * width)
        grads = []
        for k, p in enumerate(pieces):
            here = slice(k * part, (k + 1) * part)
            u = half[here] + bias_ref[here]
            t = jnp.tanh(u)
            s = 1.0 + t
            helds[k, :, at] = (u * s).astype(BF)
            c = p[cols : cols + part, at].astype(F32)
            grads.append((c * s * (1.0 + u * (1.0 - t))).astype(BF))
        return jnp.concatenate(grads, axis=0)

    def products(i, grad):
        at = slice(i * width, (i + 1) * width)
        grad_ref[:, at] = grad
        both = dot(back_w_ref[...], grad)
        backs = both[0 : 4 * cols] * inverse_ref[:, at]
        for k, b in enumerate((b0, b1, b2, b3)):
            b[:, at] = backs[k * cols : (k + 1) * cols].astype(BF)
            own = both[(4 + k) * cols : (5 + k) * cols]
            selfs[k, :, at] = own.astype(BF)

    count = rows // width
    half, grad = project(0), None
    for i in range(count):
        later = project(i + 1) if i + 1 < count else None
        fresh = gradient(i, half)
        if grad is not None:
            products(i - 1, grad)
        half, grad = later, fresh
    sends = []
    for k, h in enumerate((h0, h1, h2, h3)):
        sends.append(pltpu.make_async_copy(helds.at[k], h, sems.at[k]))
        sends[-1].start()
    products(count - 1, grad)
    for k, s in enumerate((s0, s1, s2, s3)):
        sends.append(pltpu.make_async_copy(selfs.at[k], s, sems.at[4 + k]))
        sends[-1].start()
    for send in sends:
        send.wait()


def dense(pieces, ms, inverse, down, bias, back_w):
    cols, rows = ms[0].shape
    hidden = down.shape[0]
    return call(
        dense_kernel,
        "dense",
        12 * "v" + ">vvvvvhhhhhhhh",
        (*pieces, *ms, inverse, down, bias, back_w),
        4 * (((cols, rows), BF),)
        + (((hidden, rows), BF),)
        + 4 * (((hidden // 4, rows), BF),)
        + 4 * (((cols, rows), BF),),
        scratch=[
            pltpu.VMEM((4, hidden // 4, rows), BF),
            pltpu.VMEM((4, cols, rows), BF),
            DMA((8,)),
        ],
        flops=2 * rows * hidden * 400,
    )


def after_kernel(feat_ref, p0, p1, p2, p3, m0, m1, m2, m3, grad_ref, g0, g1, g2, g3):
    cols, rows = m0.shape
    part = grad_ref.shape[0] // 4
    grad = grad_ref[...]
    left = [p[0:cols, 0:rows] for p in (p0, p1, p2, p3)] + [m[...] for m in (m0, m1, m2, m3)]
    left.append(jnp.ones((ONES, rows), BF))
    total = dot(jnp.concatenate(left, axis=0), grad, NT)
    feat = feat_ref[0]
    low, high = total[:, 0:BLK], total[:, BLK:]
    far = (feat & 2) != 0
    halves = [jnp.where(far, high, low), jnp.where(far, low, high)]
    halves = [jnp.where((feat & 1) != 0, pltpu.roll(h, part, 1), h) for h in halves]
    tall = 4 * cols
    for k, out in enumerate((g0, g1, g2, g3)):
        for h in range(2):
            at = slice(h * BLK, (h + 1) * BLK)
            out[0:cols, at] = halves[h][k * cols : (k + 1) * cols]
            out[cols : 2 * cols, at] = halves[h][tall + k * cols : tall + (k + 1) * cols]
        line = (low if k < 2 else high)[2 * tall : 2 * tall + 8]
        out[2 * cols :, 0:BLK] = pltpu.roll(line, part, 1) if k % 2 else line
        out[2 * cols :, BLK:] = jnp.zeros((8, BLK), F32)


def after(place, pieces, ms, grad):
    cols, _ = ms[0].shape
    return call(
        after_kernel,
        "after",
        "s" + 9 * "v" + ">wwww",
        (place, *pieces, *ms, grad),
        4 * (((2 * cols + 8, grad.shape[0]), F32),),
    )


def off_back_kernel(
    place_ref, row_ref, key_ref, b0, b1, b2, b3, a_ref, band_ref, out_ref, back_ref,
    held, edge_ref, sem, sems,
):
    count = band_ref.shape[0]
    edges = [
        pltpu.make_async_copy(band_ref.at[0, 0], edge_ref.at[0], sems.at[0]),
        pltpu.make_async_copy(band_ref.at[count - 1, 2], edge_ref.at[1], sems.at[1]),
    ]
    for edge in edges:
        edge.start()
    for k, b in enumerate((b0, b1, b2, b3)):
        back_ref[:, near_rows(place_ref[0], k, b.shape[1])] = b[...]
    held[...] = jnp.zeros_like(held)
    for r in range(a_ref.shape[0]):
        key = key_ref[0, r]
        left = back_ref[:, lanes(row_ref[r])]
        held[key // CAP, key % CAP] = dot(left, a_ref[r]).astype(BF)
    for edge in edges:
        edge.wait()
    below, above = [near_loop(place_ref[1], d, held.shape[0]) for d in (-1, 1)]
    rows = back_ref.shape[1]
    held[below, CAP] = dot(back_ref[:, 0:BLK], edge_ref[0]).astype(BF)
    held[above, CAP] = dot(back_ref[:, rows - BLK :], edge_ref[1]).astype(BF)
    copy = pltpu.make_async_copy(held, out_ref, sem)
    copy.start()
    copy.wait()


def off_backward(place, row, key, backs, off, band, loop_size):
    cols, part = backs[0].shape
    shape = (loop_size, SLOTS, cols, BLK)
    return call(
        off_back_kernel,
        "off_backward",
        "sssvvvvvh>hv",
        (place, row, key, *backs, off, band),
        ((shape, BF), ((cols, 4 * part), BF)),
        scratch=[pltpu.VMEM(shape, BF), pltpu.VMEM((2, BLK, BLK), BF), DMA, DMA((2,))],
    )


def band_back_kernel(back_ref, a_ref, total, held, sems):
    count, steps = a_ref.shape[0], sems.shape[0]
    group = count // steps
    copies = []
    for i in range(steps):
        at = pl.ds(i * group, group)
        copies.append(pltpu.make_async_copy(a_ref.at[at], held.at[at], sems.at[i]))
        copies[-1].start()
    carried = [None, None]
    for i in range(steps):
        copies[i].wait()
        for b in range(i * group, (i + 1) * group):
            right = jnp.concatenate([held[b, 0], held[b, 1], held[b, 2]], axis=1)
            term = dot(back_ref[:, b * BLK : (b + 1) * BLK], right)
            first, middle, last = [term[:, o * BLK : (o + 1) * BLK] for o in range(3)]
            if b > 0:
                total[:, (b - 1) * BLK : b * BLK] = carried[0] + first
            carried = [middle if b == 0 else carried[1] + middle, last]
    total[:, (count - 1) * BLK :] = carried[0]


def band_backward(back, band):
    cols, rows = back.shape
    (out,) = call(
        band_back_kernel,
        "band_backward",
        "vh>w",
        (back, band),
        (((cols, rows), F32),),
        scratch=[pltpu.VMEM(band.shape, BF), DMA((8,))],
    )
    return out


def collect_kernel(
    place_ref, asked_ref, start_ref, in_ref, h0, h1, h2, h3, s0, s1, s2, s3,
    out_ref, hidden_out, total, second, held, selfs, hidden_ref, table, sems, in_sems, out_sems,
):
    feat = place_ref[0]
    steps = in_sems.shape[0]
    group = held.shape[0] // steps

    def arrive(j):
        at = pl.ds(j * group, group)
        return pltpu.make_async_copy(in_ref.at[at], held.at[at], in_sems.at[j])

    rows, part = total.shape[1], h0.shape[1]
    copies = [
        pltpu.make_async_copy(asked_ref.at[:, 0, :], table, sems.at[0]),
        pltpu.make_async_copy(start_ref, total, sems.at[1]),
    ]
    for k, s in enumerate((s0, s1, s2, s3)):
        copies.append(pltpu.make_async_copy(s, selfs.at[k], sems.at[2 + k]))
    for k, h in enumerate((h0, h1, h2, h3)):
        at = near_rows(feat, k, part)
        copies.append(pltpu.make_async_copy(h, hidden_ref.at[:, at], sems.at[6 + k]))
    for copy in copies[:6]:
        copy.start()
    for j in range(steps):
        arrive(j).start()
    for copy in copies[6:]:
        copy.start()
    copies[1].wait()
    for k in range(4):
        copies[2 + k].wait()
        at = near_rows(feat, k, part)
        total[:, at] = total[:, at] + selfs[k].astype(F32)
    copies[0].wait()

    def body(p, carry):
        for s in range(CAP):
            at = lanes(table[p, s])
            sums = second if s % 2 else total
            sums[:, at] = sums[:, at] + held[p, s].astype(F32)
        return carry

    second[...] = jnp.zeros_like(second)
    sends = []
    for j in range(steps):
        arrive(j).wait()
        lax.fori_loop(j * group, (j + 1) * group, body, 0, unroll=4)
        copies[6 + j].wait()
        at = near_rows(feat, j, part)
        sends.append(
            pltpu.make_async_copy(hidden_ref.at[:, at], hidden_out.at[:, at], out_sems.at[j])
        )
        sends[-1].start()
    below, above = [near_loop(place_ref[1], d, held.shape[0]) for d in (-1, 1)]
    total[:, 0:BLK] += held[below, CAP].astype(F32)
    total[:, rows - BLK :] += held[above, CAP].astype(F32)
    out_ref[...] = (total[...] + second[...]).astype(BF)
    for send in sends:
        send.wait()


def collect(place, asked, band_sum, incoming, outs):
    cols, rows = band_sum.shape
    return call(
        collect_kernel,
        "collect",
        "saahhahhhahh>wh",
        (place, asked, band_sum, incoming, *outs),
        ((band_sum.shape, BF), ((outs[0].shape[0], rows), BF)),
        scratch=[
            pltpu.VMEM(band_sum.shape, F32),
            pltpu.VMEM(band_sum.shape, F32),
            pltpu.VMEM(incoming.shape, BF),
            pltpu.VMEM((4, cols, rows // 4), BF),
            pltpu.VMEM((outs[0].shape[0], rows), BF),
            pltpu.SMEM((asked.shape[0], BLK), I32),
            DMA((10,)),
            DMA((4,)),
            DMA((4,)),
        ],
    )


def finish_kernel(scale, own_ref, other_ref, out_ref, bias_ref):
    total = (own_ref[...] + other_ref[...]) * scale
    tall = out_ref.shape[0]
    out_ref[...] = total[0:tall]
    bias_ref[...] = total[tall : tall + 1, 0 : bias_ref.shape[1]]


def finish(own, other, part, scale):
    tall, wide = own.shape
    return call(
        lambda *refs: finish_kernel(scale, *refs),
        "finish",
        "ww>ww",
        (own, other),
        (((tall - 8, wide), F32), ((1, part), F32)),
    )


def per_device(
    features, band_blocks, off_blocks, off_row, off_col, off_part, w_self, w_neigh, bias, cotangent
):
    rows, cols = features.shape
    loop_size = lax.axis_size("loop")
    together = lax.optimization_barrier

    def swap(value, k, j=0):
        pairs = [(4 * i + f, 4 * (i ^ j) + (f ^ k)) for i in range(loop_size) for f in range(4)]
        return lax.ppermute(value, ("loop", "feat"), pairs)

    def swapped(values):
        return [values[0]] + [swap(values[k], k) for k in (1, 2, 3)]

    def spread(value):
        return lax.all_to_all(value, "loop", split_axis=0, concat_axis=0, tiled=True)

    place = jnp.stack([lax.axis_index("feat"), lax.axis_index("loop")]).astype(I32)
    x, cot = features.T, cotangent.T
    key, request = prepare(off_part.reshape(1, -1), off_col.reshape(1, -1), loop_size)
    request, place = together((request, place))
    asked = spread(request)
    pieces = by_device(place, x, cot, w_self, w_neigh, bias.reshape(1, -1))
    asked, then = together((asked, pieces[0]))[0], place
    pieces = swapped(pieces)
    ready = answers(place, asked, x)
    ready, then = together((ready, then))
    panels = spread(ready)
    band_sum, off = band_forward(then, band_blocks, off_blocks, x)
    *ms, inverse = off_forward(place, off_row, key, band_sum, band_blocks, panels, off)
    ms = swapped(ms)
    down, bias_down, back_w = weights(place, pieces, cols, w_self.shape[1])
    ms, down = together((ms, down))
    *rest, h0, h1, h2, h3, s0, s1, s2, s3 = dense(pieces, ms, inverse, down, bias_down, back_w)
    *backs, grad = rest
    backs = swapped(backs)
    terms = after(place, pieces, ms, grad)
    near = swapped(terms)
    selfs = [s0, s1, swap(s2, 2), swap(s3, 3)]
    outgoing, back = off_backward(place, off_row, key, backs, off, band_blocks, loop_size)
    grads = (near[0] + near[1]) + (near[2] + near[3])
    one, two, three = [swap(grads, 0, j) for j in (8, 16, 24)]
    outs = [h0, h1, h2, h3]
    grads = (grads + one) + (two + three)
    outgoing, back, grads, selfs, outs = together((outgoing, back, grads, selfs, outs))
    incoming = spread(outgoing)
    outs = [outs[0], outs[1], swap(outs[2], 2), swap(outs[3], 3)]
    back_sum = band_backward(back, band_blocks)
    one, two, three = [swap(grads, 0, j) for j in (2, 4, 6)]
    one, two, three, outs[1], selfs[1] = together((one, two, three, outs[1], selfs[1]))
    outs[1], selfs[1] = swap(outs[1], 1), swap(selfs[1], 1)
    grads = (grads + one) + (two + three)
    other = swap(grads, 0, 1)
    grad_features, hidden = collect(place, asked, back_sum, incoming, outs + selfs)
    other, grad_features = together((other, grad_features))
    weight_grads, bias_grad = finish(
        grads, other, bias.shape[0], 0.5 / math.sqrt(rows * loop_size)
    )
    return (
        hidden.T,
        grad_features.T,
        weight_grads.reshape(2, cols, w_self.shape[1]),
        bias_grad.reshape(-1),
    )


def solution(mesh):
    return jax.shard_map(
        per_device,
        mesh=mesh,
        in_specs=(
            P("loop", "feat"),
            P("loop", None, None, None),
            P("loop", None, None),
            P("loop"),
            P("loop"),
            P("loop", None),
            P("feat", None),
            P("feat", None),
            P("feat"),
            P("loop", "feat"),
        ),
        out_specs=(P("loop", "feat"), P("loop", "feat"), P(None, "feat", None), P("feat")),
        check_vma=False,
    )
```
